512 devices in a mesh: group: 8 (over x, core), dom: 64 (over z, y).
Axes of the slice: x: 4, y: 4, z: 16, core: 2. Of those that a mesh axis runs over, the one named last changes fastest.
Arguments:
- node_feats: bfloat16 [131072, 512], P(('group', 'dom')), may hold values from -40 to 40
- queries: bfloat16 [131072, 512], P(('group', 'dom')), may hold values from -240 to 240
- keys: bfloat16 [131072, 512], P(('group', 'dom')), may hold values from -6.5 to 6.5
- values: bfloat16 [131072, 512], P(('group', 'dom')), may hold values from -6 to 6
- out_weight: bfloat16 [512, 512], replicated, may hold values from -0.25 to 0.25
- up_weight: bfloat16 [512, 2048], P(None, 'group'), may hold values from -0.25 to 0.25
- down_weight: bfloat16 [512, 2048], P(None, 'group'), may hold values from -0.125 to 0.125
- norm_gain: float32 [512], replicated, may hold values from 0.5 to 1.5
- tile_lists: int32 [1024, 6], P(('group', 'dom')), may hold values from -1 to 1023, as said below
- virtual_of: int32 [131072], P(('group', 'dom')), may hold values from 0 to 63
Outputs:
- layer_out: bfloat16 [131072, 512], P(('group', 'dom'))
The draws below stay inside these ranges and needn't reach their ends.
Inputs may be any that keep to these rules, and one draw needn't show every extreme that they name: Row b of tile_lists starts with b itself, then names distinct other blocks, then -1 up to the end. Every named block c lies in the same group as b, in a partition c // 2 at most 2 away along dom from b // 2. In every draw some partitions have all of their rows full.
All inputs are finite; a program needn't handle non-finite values.
Results may differ from the reference program's by a relative error of at most 0.0095.
Values may be sent and summed in bfloat16 or wider, within the bound.
No kernel may reach another device: no remote copies, remote signals or barrier semaphores. Data moves between devices by JAX's collectives and lax.ppermute only.
A program may use at most 64 MiB of HBM per device.

```python
import math
import jax
import jax.numpy as jnp
from jax import lax

D = 512
HEADS = 8
FF = 2048
BLOCK = 128
VIRTUAL = 64
REACH = 2
TMAX = 6
BLOCKS_DEV = 2
NODE_DEV = 256
NODES = 131072
QBLOCKS = 1024
N_DOM = 64


def shared_normal(key):
    return jnp.clip(jax.random.normal(key, (NODES, D), jnp.float32), -6.0, 6.0)


def draw_keys(key, part):
    shared = shared_normal(key)
    return shared.astype(jnp.bfloat16)


def draw_queries(key, part):
    key = jax.random.fold_in(key, 7)
    own_part = jnp.clip(jax.random.normal(key, (NODES, D), jnp.float32), -6.0, 6.0)
    return own_part.astype(jnp.bfloat16)


def draw_node_feats(key, part):
    key = jax.random.fold_in(key, 9)
    first_key = jax.random.fold_in(key, 0)
    normal_part = jnp.clip(jax.random.normal(first_key, (NODES, D), jnp.float32), -6.0, 6.0)
    return normal_part.astype(jnp.bfloat16)


def draw_tile_lists(key, part):
    key = jax.random.fold_in(key, 5)
    score_key, count_key, phase_key = jax.random.split(key, 3)
    window_width = (2 * REACH + 1) * BLOCKS_DEV
    block_ids = jnp.arange(QBLOCKS, dtype=jnp.int32)
    device_ids = block_ids // BLOCKS_DEV
    dom_ids = device_ids % N_DOM
    slot_ids = jnp.arange(window_width, dtype=jnp.int32)
    offset_ids = slot_ids // BLOCKS_DEV - REACH
    candidates = (device_ids[:, None] + offset_ids[None, :]) * BLOCKS_DEV + (slot_ids % BLOCKS_DEV)[None, :]
    target_dom = dom_ids[:, None] + offset_ids[None, :]
    usable = (target_dom >= 0) & (target_dom < N_DOM) & (candidates != block_ids[:, None])
    raw_scores = jax.random.randint(score_key, (QBLOCKS, window_width), 0, 65536, jnp.int32) * window_width + slot_ids[None, :]
    raw_scores = jnp.where(usable, raw_scores, -1)
    unused_values, picked = lax.top_k(raw_scores, TMAX - 1)
    chosen = jnp.take_along_axis(candidates, picked, axis=1)
    base_count = jax.random.randint(count_key, (QBLOCKS,), 1, TMAX // 2 + 1, jnp.int32)
    phase = jax.random.randint(phase_key, (), 0, 16, jnp.int32)
    full_rows = device_ids % 16 == phase
    tile_count = jnp.where(full_rows, TMAX, base_count)
    slot_rank = jnp.arange(TMAX - 1, dtype=jnp.int32)
    chosen = jnp.where(slot_rank[None, :] < (tile_count - 1)[:, None], chosen, -1)
    return jnp.concatenate([block_ids[:, None], chosen], axis=1).astype(jnp.int32)


def set_ends(values, stream_key, least, top_value):
    place = [jax.random.randint(jax.random.fold_in(stream_key, axis), (), 0, length) for axis, length in enumerate(values.shape)]
    main_axis = values.shape.index(max(values.shape))
    next_to = place[:main_axis] + [(place[main_axis] + 1) % values.shape[main_axis]] + place[main_axis + 1:]
    return values.at[tuple(place)].set(least).at[tuple(next_to)].set(top_value)


def shard_levels(key, extent, cuts, smallest, largest):
    loudness, own = 1.0, jax.random.fold_in(key, 6)
    for axis_at, shards_of in cuts:
        heights = jnp.exp(jax.random.uniform(jax.random.fold_in(own, axis_at), (shards_of,), jnp.float32, smallest / len(cuts), largest / len(cuts)))
        loudness = loudness * jnp.repeat(heights, extent[axis_at] // shards_of).reshape([-1 if axis == axis_at else 1 for axis in range(len(extent))])
    return loudness


def scatter_about(own_key, shape, width, reach, pieces=(), kind=jnp.bfloat16):
    factor_of = shard_levels(own_key, shape, pieces, -0.22, 0.18) if pieces else 1.0
    values = jax.random.normal(own_key, shape, jnp.float32) * width * factor_of
    return jnp.minimum(jnp.maximum(values, -reach), reach).astype(kind)


def setup_inputs(seed: int = 0) -> dict:
    arg_keys = jax.random.split(jax.random.key(seed), 11)
    return {
        "node_feats": draw_node_feats(jax.random.fold_in(arg_keys[10], 71), 0),
        "queries": draw_queries(jax.random.fold_in(arg_keys[10], 71), 0),
        "keys": draw_keys(jax.random.fold_in(arg_keys[10], 71), 0),
        "values": scatter_about(arg_keys[3], (NODES, D), 1.0, 6.0, ((0, 512),)),
        "out_weight": scatter_about(arg_keys[4], (D, D), D ** -0.5, 0.25),
        "up_weight": scatter_about(arg_keys[5], (D, FF), D ** -0.5, 0.25, ((1, 8),)),
        "down_weight": scatter_about(arg_keys[6], (D, FF), FF ** -0.5, 0.125, ((1, 8),)),
        "norm_gain": jnp.clip(1.0 + 0.1 * jax.random.normal(arg_keys[7], (D,), jnp.float32), 0.5, 1.5),
        "tile_lists": draw_tile_lists(jax.random.fold_in(arg_keys[10], 71), 0),
        "virtual_of": set_ends(jax.random.randint(arg_keys[9], (NODES,), 0, VIRTUAL), jax.random.fold_in(arg_keys[9], 1), 0, VIRTUAL - 1).astype(jnp.int32),
    }


def reference(node_feats, queries, keys, values, out_weight, up_weight, down_weight, norm_gain, tile_lists, virtual_of):
    head_dim = D // HEADS
    score_scale = 1.0 / math.sqrt(head_dim)
    members = (virtual_of[None, :] == jnp.arange(VIRTUAL, dtype=jnp.int32)[:, None]).astype(jnp.bfloat16)
    pool_scale = math.sqrt(VIRTUAL / NODES)
    virtual_keys = (jnp.dot(members, keys, preferred_element_type=jnp.float32) * pool_scale).astype(jnp.bfloat16)
    virtual_values = (jnp.dot(members, values, preferred_element_type=jnp.float32) * pool_scale).astype(jnp.bfloat16)
    key_blocks = keys.reshape(QBLOCKS, BLOCK, D)
    value_blocks = values.reshape(QBLOCKS, BLOCK, D)
    query_blocks = queries.reshape(QBLOCKS, BLOCK, HEADS, head_dim)
    virtual_key_heads = virtual_keys.astype(jnp.float32).reshape(VIRTUAL, HEADS, head_dim)
    virtual_value_heads = virtual_values.astype(jnp.float32).reshape(VIRTUAL, HEADS, head_dim)

    def attend(inputs):
        query, listed = inputs
        present = listed >= 0
        picked = jnp.where(present, listed, 0).astype(jnp.int32)
        near_keys = key_blocks[picked].reshape(TMAX * BLOCK, HEADS, head_dim).astype(jnp.float32)
        near_values = value_blocks[picked].reshape(TMAX * BLOCK, HEADS, head_dim).astype(jnp.float32)
        all_keys = jnp.concatenate([near_keys, virtual_key_heads], axis=0)
        all_values = jnp.concatenate([near_values, virtual_value_heads], axis=0)
        allowed = jnp.concatenate([jnp.repeat(present, BLOCK), jnp.ones((VIRTUAL,), dtype=bool)])
        scores = jnp.einsum('qhd,khd->hqk', query.astype(jnp.float32), all_keys) * score_scale
        scores = jnp.where(allowed[None, None, :], scores, -jnp.inf)
        row_max = lax.optimization_barrier(jnp.max(scores, axis=-1, keepdims=True))
        exponent = jnp.exp(scores - row_max)
        denominator = lax.optimization_barrier(jnp.sum(exponent, axis=-1))
        weights = lax.optimization_barrier(exponent.astype(jnp.bfloat16)).astype(jnp.float32)
        summed = jnp.einsum('hqk,khd->hqd', weights, all_values)
        result = summed / denominator[..., None]
        return jnp.transpose(result, (1, 0, 2)).reshape(BLOCK, D).astype(jnp.bfloat16)
    attended = lax.map(attend, (query_blocks, tile_lists)).reshape(NODES, D)

    def finish(inputs):
        feats, attn_rows = inputs
        residual = feats.astype(jnp.float32) + jnp.dot(attn_rows, out_weight, preferred_element_type=jnp.float32)
        row_mean = lax.optimization_barrier(jnp.mean(residual, axis=-1, keepdims=True))
        centered = residual - row_mean
        variance = lax.optimization_barrier(jnp.mean(centered * centered, axis=-1, keepdims=True))
        normed = (centered * lax.rsqrt(variance + 1e-05) * norm_gain).astype(jnp.bfloat16)
        hidden = jax.nn.relu(jnp.dot(normed, up_weight, preferred_element_type=jnp.float32)).astype(jnp.bfloat16)
        ffn_out = lax.dot_general(hidden, down_weight, (((1,), (1,)), ((), ())), preferred_element_type=jnp.float32)
        return (residual + ffn_out).astype(jnp.bfloat16)
    layer_out = lax.map(finish, (node_feats.reshape(-1, NODE_DEV, D), attended.reshape(-1, NODE_DEV, D)))
    return layer_out.reshape(NODES, D)
```

```python
import math

import jax
import jax.numpy as jnp
from jax import lax
from jax.experimental import pallas as pl
from jax.experimental.pallas import tpu as pltpu
from jax.sharding import Mesh
from jax.sharding import PartitionSpec as P

HEADS = 8
BLOCK = 128
VIRTUAL = 64
REACH = 2
TMAX = 6
LANES = 128
LOG2E = 1.4426950408889634
AXES = ("x", "c", "z", "y")
DOM = ("z", "y")
PLANE = ("x", "c", "y")
VMEM = pltpu.VMEM
F32 = jnp.float32
BF16 = jnp.bfloat16


def pool_kernel(virtual_of, keys, values, up, down, sums, key_value, weights):
    node_rows, feat_width = keys.shape
    ids = lax.broadcasted_iota(jnp.int32, (VIRTUAL, node_rows), 0)
    members = jnp.where(virtual_of[...] == ids, 1.0, 0.0).astype(BF16)
    per_part = sums.shape[1]
    lane_parts = feat_width // LANES
    rows_parts = VIRTUAL // per_part
    for which, source in enumerate((keys, values)):
        pooled = jnp.dot(members, source[...], preferred_element_type=F32)
        for row in range(rows_parts):
            for lane in range(lane_parts):
                sums[(which * rows_parts + row) * lane_parts + lane] = pooled[
                    row * per_part : (row + 1) * per_part, lane * LANES : (lane + 1) * LANES
                ]
        key_value[which] = source[...]
    weights[0] = up[...]
    weights[1] = down[...]


def layer_kernel(
    tile_lists,
    queries,
    node_feats,
    out_weight,
    norm_gain,
    virtual_kv,
    kv_m2,
    kv_m1,
    kv_0,
    kv_p1,
    kv_p2,
    w_0,
    w_1,
    w_2,
    w_3,
    w_far,
    layer_out,
    window,
    weights,
    kv_sem,
    w_sem,
    attended,
):
    feat_width = queries.shape[1]
    head_dim = feat_width // HEADS
    pieces = (kv_m2, kv_m1, kv_0, kv_p1, kv_p2)
    rows = kv_0.shape[1]
    copies = [
        pltpu.make_async_copy(piece, window.at[:, pl.ds(i * rows, rows)], kv_sem.at[i])
        for i, piece in enumerate(pieces)
    ]
    near = (w_0, w_1, w_2, w_3)
    w_copies = [
        pltpu.make_async_copy(piece, weights.at[i], w_sem.at[i]) for i, piece in enumerate(near)
    ]
    w_copies.append(
        pltpu.make_async_copy(w_far, weights.at[pl.ds(len(near), len(near))], w_sem.at[len(near)])
    )
    for copy in copies:
        copy.start()
    for copy in w_copies:
        copy.start()
    for copy in copies:
        copy.wait()

    first_block = tile_lists[0, 0] - REACH * (rows // BLOCK)
    scale = LOG2E / math.sqrt(head_dim)
    lane_parts = feat_width // LANES
    per_part = virtual_kv.shape[1]
    rows_parts = VIRTUAL // per_part
    low = lax.broadcasted_iota(jnp.int32, (BLOCK, LANES), 1) < head_dim
    for block in range(rows // BLOCK):
        own = tile_lists[block, 0]
        starts = []
        shown = []
        for slot in range(TMAX):
            tile = tile_lists[block, slot]
            there = tile >= 0
            place = jnp.where(there, tile, own) - first_block
            starts.append(pl.multiple_of(place * BLOCK, BLOCK))
            shown.append(jnp.where(there, 1.0, 0.0))
        for part in range(lane_parts):
            lanes = slice(part * LANES, (part + 1) * LANES)
            pair = queries[block * BLOCK : (block + 1) * BLOCK, lanes]
            zero = jnp.zeros_like(pair)
            both = jnp.concatenate([jnp.where(low, pair, zero), jnp.where(low, zero, pair)], axis=0)
            all_keys = jnp.concatenate(
                [window[0, pl.ds(s, BLOCK), lanes] for s in starts]
                + [virtual_kv[r * lane_parts + part] for r in range(rows_parts)],
                axis=0,
            )
            scores = lax.dot_general(
                both, all_keys, (((1,), (1,)), ((), ())), preferred_element_type=F32
            )
            row_max = jnp.max(scores, axis=-1, keepdims=True)
            exponent = jnp.exp2(scores * scale - row_max * scale).astype(BF16)
            value_rows = [window[1, pl.ds(s, BLOCK), lanes] for s in starts]
            ones = [jnp.full((BLOCK, LANES), there, F32).astype(BF16) for there in shown]
            value_rows = [v * o for v, o in zip(value_rows, ones)]
            value_rows += [
                virtual_kv[(rows_parts + r) * lane_parts + part] for r in range(rows_parts)
            ]
            ones.append(jnp.ones((VIRTUAL, LANES), BF16))
            right = jnp.concatenate(
                [jnp.concatenate(value_rows, axis=0), jnp.concatenate(ones, axis=0)], axis=1
            )
            summed = jnp.dot(exponent, right, preferred_element_type=F32)
            result = summed[:, :LANES] / summed[:, LANES:]
            attended[block * BLOCK : (block + 1) * BLOCK, lanes] = jnp.where(
                low, result[:BLOCK], result[BLOCK:]
            ).astype(BF16)

    residual = node_feats[...].astype(F32) + jnp.dot(
        attended[...], out_weight[...], preferred_element_type=F32
    )
    row_mean = jnp.mean(residual, axis=-1, keepdims=True)
    centered = residual - row_mean
    variance = jnp.mean(centered * centered, axis=-1, keepdims=True)
    normed = (centered * lax.rsqrt(variance + 1e-05) * norm_gain[...]).astype(BF16)
    for copy in w_copies:
        copy.wait()
    total = residual
    for shard in range(2 * len(near)):
        hidden = jnp.dot(normed, weights[shard, 0], preferred_element_type=F32)
        hidden = jnp.maximum(hidden, 0.0).astype(BF16)
        total = total + lax.dot_general(
            hidden, weights[shard, 1], (((1,), (1,)), ((), ())), preferred_element_type=F32
        )
    layer_out[...] = total.astype(BF16)


def along_dom(shard, by):
    length = lax.axis_size(DOM)
    pairs = [(i, i + by) for i in range(length) if 0 <= i + by < length]
    return lax.ppermute(shard, DOM, pairs)


def around(shard, axis, by):
    length = lax.axis_size(axis)
    return lax.ppermute(shard, axis, [(i, (i + by) % length) for i in range(length)])


def exchanged(parts, axes):
    return lax.all_to_all(parts, axes, 0, 0, tiled=True)


def local(
    node_feats,
    queries,
    keys,
    values,
    out_weight,
    up_weight,
    down_weight,
    norm_gain,
    tile_lists,
    virtual_of,
):
    node_rows, feat_width = queries.shape
    plane = lax.axis_size(PLANE)
    depth = lax.axis_size("z")
    per_part = 2 * VIRTUAL * feat_width // LANES // plane
    own_hidden = up_weight.shape[1]
    in_vmem = pl.BlockSpec(memory_space=VMEM)
    anywhere = pl.BlockSpec(memory_space=pl.ANY)
    sums, key_value, w_0 = pl.pallas_call(
        pool_kernel,
        out_shape=(
            jax.ShapeDtypeStruct((plane, per_part, LANES), F32),
            jax.ShapeDtypeStruct((2, node_rows, feat_width), BF16),
            jax.ShapeDtypeStruct((2, feat_width, own_hidden), BF16),
        ),
        in_specs=[in_vmem] * 5,
        out_specs=(in_vmem,) * 3,
        name="pool",
    )(virtual_of.reshape(1, node_rows), keys, values, up_weight, down_weight)

    pieces = {offset: along_dom(key_value, -offset) for offset in (-1, 1, -2, 2)}
    w_1 = around(w_0, "x", 1)
    w_2 = around(w_0, "x", -1)
    w_3 = around(w_0, "x", 2)
    w_far = around(jnp.stack([w_0, w_1, w_2, w_3]), "c", 1)

    plane_sum = jnp.sum(exchanged(sums, PLANE), axis=0, keepdims=True)
    everywhere = exchanged(jnp.broadcast_to(plane_sum, (depth, per_part, LANES)), "z")
    pool_scale = math.sqrt(VIRTUAL / (node_rows * lax.axis_size(AXES)))
    pooled = (jnp.sum(everywhere, axis=0, keepdims=True) * pool_scale).astype(BF16)
    virtual_kv = exchanged(jnp.broadcast_to(pooled, (plane, per_part, LANES)), PLANE)

    return pl.pallas_call(
        layer_kernel,
        out_shape=jax.ShapeDtypeStruct((node_rows, feat_width), BF16),
        in_specs=[pl.BlockSpec(memory_space=pltpu.SMEM)] + [in_vmem] * 5 + [anywhere] * 10,
        out_specs=in_vmem,
        scratch_shapes=[
            VMEM((2, (2 * REACH + 1) * node_rows, feat_width), BF16),
            VMEM((8, 2, feat_width, own_hidden), BF16),
            pltpu.SemaphoreType.DMA((2 * REACH + 1,)),
            pltpu.SemaphoreType.DMA((5,)),
            VMEM((node_rows, feat_width), BF16),
        ],
        compiler_params=pltpu.CompilerParams(vmem_limit_bytes=32 * 1024 * 1024),
        name="layer",
    )(
        tile_lists,
        queries,
        node_feats,
        out_weight,
        norm_gain.reshape(1, feat_width),
        virtual_kv,
        pieces[-2],
        pieces[-1],
        key_value,
        pieces[1],
        pieces[2],
        w_0,
        w_1,
        w_2,
        w_3,
        w_far,
    )


def solution(mesh):
    group, dom = mesh.devices.shape
    fine = Mesh(mesh.devices.reshape(group // 2, 2, dom // 4, 4), AXES)
    placed = (
        P(AXES, None),
        P(AXES, None),
        P(AXES, None),
        P(AXES, None),
        P(),
        P(None, ("x", "c")),
        P(None, ("x", "c")),
        P(),
        P(AXES, None),
        P(AXES),
    )
    return jax.shard_map(
        local, mesh=fine, in_specs=placed, out_specs=P(AXES, None), check_vma=False
    )
```

```python
import functools
import math

import jax
import jax.numpy as jnp
from jax import lax
from jax.experimental import pallas as pl
from jax.experimental.pallas import tpu as pltpu
from jax.sharding import Mesh
from jax.sharding import PartitionSpec as P

HEADS = 8
BLOCK = 128
VIRTUAL = 64
REACH = 2
TMAX = 6
LANES = 128
LOG2E = 1.4426950408889634
AXES = ("x", "c", "z", "y")
DOM = ("z", "y")
PLANE = ("x", "c", "y")
VMEM = pltpu.VMEM
F32 = jnp.float32
BF16 = jnp.bfloat16


def pool_kernel(
    virtual_of_in, keys_in, values_in, up_in, down_in, sums, key_value, weights, virtual_of, sem
):
    copies = [
        pltpu.make_async_copy(source, target, sem.at[i])
        for i, (source, target) in enumerate(
            (
                (virtual_of_in, virtual_of),
                (keys_in, key_value.at[0]),
                (values_in, key_value.at[1]),
                (up_in, weights.at[0]),
                (down_in, weights.at[1]),
            )
        )
    ]
    for copy in copies:
        copy.start()
    for copy in copies[:3]:
        copy.wait()
    node_rows, feat_width = key_value.shape[1:]
    ids = lax.broadcasted_iota(jnp.int32, (VIRTUAL, node_rows), 0)
    members = jnp.where(virtual_of[...] == ids, 1.0, 0.0).astype(BF16)
    per_part = sums.shape[1]
    lane_parts = feat_width // LANES
    rows_parts = VIRTUAL // per_part
    for which in range(2):
        pooled = jnp.dot(members, key_value[which], preferred_element_type=F32)
        for row in range(rows_parts):
            for lane in range(lane_parts):
                sums[(which * rows_parts + row) * lane_parts + lane] = pooled[
                    row * per_part : (row + 1) * per_part, lane * LANES : (lane + 1) * LANES
                ]
    for copy in copies[3:]:
        copy.wait()


def plane_sum_kernel(parts, total):
    total[...] = jnp.broadcast_to(jnp.sum(parts[...], axis=0, keepdims=True), total.shape)


def pooled_kernel(scale, parts, after, pooled):
    mean = (jnp.sum(parts[...], axis=0, keepdims=True) * scale).astype(BF16)
    pooled[...] = jnp.broadcast_to(mean, pooled.shape)


def stack_kernel(after, w_0, w_1, w_2, w_3, stacked):
    for i, piece in enumerate((w_0, w_1, w_2, w_3)):
        stacked[i] = piece[...]


def head_pair(queries, block, lanes, low):
    pair = queries[block * BLOCK : (block + 1) * BLOCK, lanes]
    zero = jnp.zeros_like(pair)
    return jnp.concatenate([jnp.where(low, pair, zero), jnp.where(low, zero, pair)], axis=0)


def attend(both, keys, values, ones, bias, scale, low):
    scores = lax.dot_general(both, keys, (((1,), (1,)), ((), ())), preferred_element_type=F32)
    scores = scores * scale
    if bias is not None:
        scores = scores + bias
    row_max = jnp.max(scores, axis=-1, keepdims=True)
    exponent = jnp.exp2(scores - row_max).astype(BF16)
    right = jnp.concatenate([values, ones], axis=1)
    summed = jnp.dot(exponent, right, preferred_element_type=F32)
    top, bottom = summed[:BLOCK], summed[BLOCK:]
    numerator = jnp.where(low, top[:, :LANES], bottom[:, :LANES])
    denominator = jnp.where(low, top[:, LANES:], bottom[:, LANES:])
    return numerator, denominator, jnp.where(low, row_max[:BLOCK], row_max[BLOCK:])


def named(tile_lists, block, place, first_block):
    wanted = first_block + place
    found = tile_lists[block, 0] == wanted
    for slot in range(1, TMAX):
        found = jnp.logical_or(found, tile_lists[block, slot] == wanted)
    return jnp.logical_and(found, wanted >= 0)


def near_kernel(
    tile_lists,
    after,
    queries_in,
    keys,
    values,
    kv_m1,
    kv_p1,
    numerators,
    denominators,
    maxima,
    queries,
    window,
    sem,
):
    rows, feat_width = queries.shape
    head_dim = feat_width // HEADS
    copies = [
        pltpu.make_async_copy(queries_in, queries, sem.at[0]),
        pltpu.make_async_copy(keys, window.at[0, pl.ds(rows, rows)], sem.at[1]),
        pltpu.make_async_copy(values, window.at[1, pl.ds(rows, rows)], sem.at[2]),
        pltpu.make_async_copy(kv_m1, window.at[:, pl.ds(0, rows)], sem.at[3]),
        pltpu.make_async_copy(kv_p1, window.at[:, pl.ds(2 * rows, rows)], sem.at[4]),
    ]
    for copy in copies:
        copy.start()
    for copy in copies:
        copy.wait()
    blocks = rows // BLOCK
    first_block = tile_lists[0, 0] - blocks
    scale = LOG2E / math.sqrt(head_dim)
    low = lax.broadcasted_iota(jnp.int32, (BLOCK, LANES), 1) < head_dim
    for block in range(blocks):
        own = tile_lists[block, 0] - first_block
        starts = []
        shown = []
        for place in range(3 * blocks):
            there = named(tile_lists, block, place, first_block)
            starts.append(pl.multiple_of(jnp.where(there, place, own) * BLOCK, BLOCK))
            shown.append(jnp.full((BLOCK, LANES), jnp.where(there, 1.0, 0.0), F32).astype(BF16))
        for part in range(feat_width // LANES):
            lanes = slice(part * LANES, (part + 1) * LANES)
            keys_here = [window[0, pl.ds(s, BLOCK), lanes] for s in starts]
            values_here = [window[1, pl.ds(s, BLOCK), lanes] * o for s, o in zip(starts, shown)]
            numerator, denominator, row_max = attend(
                head_pair(queries, block, lanes, low),
                jnp.concatenate(keys_here, axis=0),
                jnp.concatenate(values_here, axis=0),
                jnp.concatenate(shown, axis=0),
                None,
                scale,
                low,
            )
            here = slice(block * BLOCK, (block + 1) * BLOCK)
            numerators[here, lanes] = numerator
            denominators[here, lanes] = denominator
            maxima[here, lanes] = row_max


def layer_kernel(
    tile_lists,
    virtual_kv,
    numerators_in,
    denominators_in,
    maxima_in,
    queries_in,
    node_feats_in,
    out_weight_in,
    norm_gain_in,
    kv_m2,
    kv_p2,
    w_near_in,
    partial_out,
    normed_out,
    window,
    numerators,
    denominators,
    maxima,
    queries,
    node_feats,
    out_weight,
    norm_gain,
    w_near,
    attended,
    sem,
):
    rows, feat_width = queries.shape
    copies = [
        pltpu.make_async_copy(source, target, sem.at[i])
        for i, (source, target) in enumerate(
            (
                (queries_in, queries),
                (kv_m2, window.at[:, pl.ds(0, rows)]),
                (kv_p2, window.at[:, pl.ds(rows, rows)]),
                (numerators_in, numerators),
                (denominators_in, denominators),
                (maxima_in, maxima),
                (out_weight_in, out_weight),
                (node_feats_in, node_feats),
                (norm_gain_in, norm_gain),
                (w_near_in, w_near),
            )
        )
    ]
    for copy in copies:
        copy.start()
    for copy in copies[:6]:
        copy.wait()
    head_dim = feat_width // HEADS
    scale = LOG2E / math.sqrt(head_dim)
    lane_parts = feat_width // LANES
    rows_parts = VIRTUAL // virtual_kv.shape[1]
    blocks = rows // BLOCK
    far_blocks = 2 * blocks
    low = lax.broadcasted_iota(jnp.int32, (BLOCK, LANES), 1) < head_dim
    ones = jnp.ones((far_blocks * BLOCK + VIRTUAL, LANES), BF16)
    first_block = tile_lists[0, 0] - 2 * blocks
    for block in range(blocks):
        here = slice(block * BLOCK, (block + 1) * BLOCK)
        bias = [
            jnp.full(
                (1, BLOCK),
                jnp.where(
                    named(tile_lists, block, place + (3 * blocks if place >= blocks else 0), first_block),
                    0.0,
                    -jnp.inf,
                ),
                F32,
            )
            for place in range(far_blocks)
        ]
        bias = jnp.concatenate(bias + [jnp.zeros((1, VIRTUAL), F32)], axis=1)
        for part in range(lane_parts):
            lanes = slice(part * LANES, (part + 1) * LANES)
            pooled = [virtual_kv[r * lane_parts + part] for r in range(2 * rows_parts)]
            numerator, denominator, row_max = attend(
                head_pair(queries, block, lanes, low),
                jnp.concatenate([window[0, :, lanes]] + pooled[:rows_parts], axis=0),
                jnp.concatenate([window[1, :, lanes]] + pooled[rows_parts:], axis=0),
                ones,
                bias,
                scale,
                low,
            )
            near_max = maxima[here, lanes]
            top = jnp.maximum(near_max, row_max)
            keep = jnp.exp2(near_max - top)
            add = jnp.exp2(row_max - top)
            attended[here, lanes] = (
                (numerators[here, lanes] * keep + numerator * add)
                / (denominators[here, lanes] * keep + denominator * add)
            ).astype(BF16)

    for copy in copies[6:9]:
        copy.wait()
    residual = node_feats[...].astype(F32) + jnp.dot(
        attended[...], out_weight[...], preferred_element_type=F32
    )
    row_mean = jnp.mean(residual, axis=-1, keepdims=True)
    centered = residual - row_mean
    variance = jnp.mean(centered * centered, axis=-1, keepdims=True)
    normed = (centered * lax.rsqrt(variance + 1e-05) * norm_gain[...]).astype(BF16)
    normed_out[...] = normed
    copies[9].wait()
    partial_out[...] = residual + hidden_sum(normed, w_near)


def hidden_sum(normed, weights):
    total = 0.0
    for shard in range(weights.shape[0]):
        hidden = jnp.dot(normed, weights[shard, 0], preferred_element_type=F32)
        hidden = jnp.maximum(hidden, 0.0).astype(BF16)
        total = total + lax.dot_general(
            hidden, weights[shard, 1], (((1,), (1,)), ((), ())), preferred_element_type=F32
        )
    return total


def finish_kernel(partial, normed, weights, layer_out):
    layer_out[...] = (partial[...] + hidden_sum(normed[...], weights)).astype(BF16)


def along_dom(shard, by):
    length = lax.axis_size(DOM)
    pairs = [(i, i + by) for i in range(length) if 0 <= i + by < length]
    return lax.ppermute(shard, DOM, pairs)


def around(shard, axis, by):
    length = lax.axis_size(axis)
    return lax.ppermute(shard, axis, [(i, (i + by) % length) for i in range(length)])


def exchanged(parts, axes):
    return lax.all_to_all(parts, axes, 0, 0, tiled=True)


def local(
    node_feats,
    queries,
    keys,
    values,
    out_weight,
    up_weight,
    down_weight,
    norm_gain,
    tile_lists,
    virtual_of,
):
    node_rows, feat_width = queries.shape
    plane = lax.axis_size(PLANE)
    depth = lax.axis_size("z")
    near = lax.axis_size("x")
    per_part = 2 * VIRTUAL * feat_width // LANES // plane
    own_hidden = up_weight.shape[1]
    in_vmem = pl.BlockSpec(memory_space=VMEM)
    in_smem = pl.BlockSpec(memory_space=pltpu.SMEM)
    anywhere = pl.BlockSpec(memory_space=pl.ANY)
    shape = jax.ShapeDtypeStruct

    def grant(mib):
        return pltpu.CompilerParams(vmem_limit_bytes=mib * 1024 * 1024)

    def hbm(array):
        return pltpu.with_memory_space_constraint(array, pltpu.HBM)

    def dma(count):
        return pltpu.SemaphoreType.DMA((count,))

    kv_shape = (2, node_rows, feat_width)
    w_shape = (2, feat_width, own_hidden)
    sums, key_value, w_0 = pl.pallas_call(
        pool_kernel,
        out_shape=(
            shape((plane, per_part, LANES), F32),
            pltpu.HBM(kv_shape, BF16),
            pltpu.HBM(w_shape, BF16),
        ),
        in_specs=[anywhere] * 5,
        out_specs=(in_vmem,) * 3,
        scratch_shapes=[VMEM((1, node_rows), jnp.int32), dma(5)],
        compiler_params=grant(6),
        name="pool",
    )(
        hbm(virtual_of.reshape(1, node_rows)),
        hbm(keys),
        hbm(values),
        hbm(up_weight),
        hbm(down_weight),
    )
    parts = exchanged(sums, PLANE)
    kv_m1 = along_dom(key_value, 1)
    kv_p1 = along_dom(key_value, -1)
    w_1 = around(w_0, "x", 1)
    w_2 = around(w_0, "x", -1)
    w_3 = around(w_0, "x", 2)

    plane_sum = pl.pallas_call(
        plane_sum_kernel,
        out_shape=shape((depth, per_part, LANES), F32),
        in_specs=[in_vmem],
        out_specs=in_vmem,
        compiler_params=grant(2),
        name="plane_sum",
    )(parts)

    parts = exchanged(plane_sum, "z")
    kv_m2 = along_dom(kv_m1, 1)
    kv_p2 = along_dom(kv_p1, -1)
    wide = pltpu.HBM((node_rows, feat_width), F32)
    nears = pl.pallas_call(
        near_kernel,
        out_shape=(wide, wide, wide),
        in_specs=[in_smem] + [anywhere] * 6,
        out_specs=(in_vmem,) * 3,
        scratch_shapes=[
            VMEM((node_rows, feat_width), BF16),
            VMEM((2, 3 * node_rows, feat_width), BF16),
            dma(5),
        ],
        compiler_params=grant(12),
        cost_estimate=pl.CostEstimate(
            flops=4_000_000_000, bytes_accessed=6_000_000, transcendentals=2_000_000
        ),
        name="near",
    )(tile_lists, plane_sum, hbm(queries), hbm(keys), hbm(values), kv_m1, kv_p1)

    pool_scale = math.sqrt(VIRTUAL / (node_rows * lax.axis_size(AXES)))
    pooled = pl.pallas_call(
        functools.partial(pooled_kernel, pool_scale),
        out_shape=shape((plane, per_part, LANES), BF16),
        in_specs=[in_vmem, anywhere],
        out_specs=in_vmem,
        compiler_params=grant(2),
        name="pooled",
    )(parts, hbm(nears[2]))

    virtual_kv = exchanged(pooled, PLANE)
    w_near = pl.pallas_call(
        stack_kernel,
        out_shape=pltpu.HBM((near, *w_shape), BF16),
        in_specs=[anywhere] + [in_vmem] * near,
        out_specs=in_vmem,
        compiler_params=grant(6),
        name="stack",
    )(pooled, hbm(w_0), w_1, w_2, w_3)
    w_far = around(w_near, "c", 1)

    partial, normed = pl.pallas_call(
        layer_kernel,
        out_shape=(wide, shape((node_rows, feat_width), BF16)),
        in_specs=[in_smem, in_vmem] + [anywhere] * 10,
        out_specs=(in_vmem,) * 2,
        scratch_shapes=[
            VMEM((2, 2 * node_rows, feat_width), BF16),
            VMEM((node_rows, feat_width), F32),
            VMEM((node_rows, feat_width), F32),
            VMEM((node_rows, feat_width), F32),
            VMEM((node_rows, feat_width), BF16),
            VMEM((node_rows, feat_width), BF16),
            VMEM(out_weight.shape, BF16),
            VMEM((1, feat_width), F32),
            VMEM((near, *w_shape), BF16),
            VMEM((node_rows, feat_width), BF16),
            dma(10),
        ],
        compiler_params=grant(20),
        cost_estimate=pl.CostEstimate(
            flops=400_000_000_000, bytes_accessed=6_000_000, transcendentals=2_000_000
        ),
        name="layer",
    )(
        tile_lists,
        virtual_kv,
        *[hbm(part) for part in nears],
        hbm(queries),
        hbm(node_feats),
        hbm(out_weight),
        hbm(norm_gain.reshape(1, feat_width)),
        kv_m2,
        kv_p2,
        hbm(w_near),
    )
    return pl.pallas_call(
        finish_kernel,
        out_shape=shape((node_rows, feat_width), BF16),
        in_specs=[in_vmem] * 3,
        out_specs=in_vmem,
        compiler_params=grant(10),
        name="finish",
    )(hbm(partial), normed, w_far)


def solution(mesh):
    group, dom = mesh.devices.shape
    fine = Mesh(mesh.devices.reshape(group // 2, 2, dom // 4, 4), AXES)
    placed = (
        P(AXES, None),
        P(AXES, None),
        P(AXES, None),
        P(AXES, None),
        P(),
        P(None, ("x", "c")),
        P(None, ("x", "c")),
        P(),
        P(AXES, None),
        P(AXES),
    )
    return jax.shard_map(
        local, mesh=fine, in_specs=placed, out_specs=P(AXES, None), check_vma=False
    )
```

```python
import functools
import math

import jax
import jax.numpy as jnp
from jax import lax
from jax.experimental import pallas as pl
from jax.experimental.pallas import tpu as pltpu
from jax.sharding import Mesh
from jax.sharding import PartitionSpec as P

HEADS = 8
BLOCK = 128
VIRTUAL = 64
REACH = 2
TMAX = 6
LANES = 128
LOG2E = 1.4426950408889634
AXES = ("x", "c", "z", "y")
DOM = ("z", "y")
PLANE = ("x", "c", "y")
VMEM = pltpu.VMEM
F32 = jnp.float32
BF16 = jnp.bfloat16


def pool_kernel(
    virtual_of_in, keys_in, values_in, up_in, down_in, sums, key_value, weights, virtual_of, sem
):
    copies = [
        pltpu.make_async_copy(source, target, sem.at[i])
        for i, (source, target) in enumerate(
            (
                (virtual_of_in, virtual_of),
                (keys_in, key_value.at[0]),
                (values_in, key_value.at[1]),
                (up_in, weights.at[0]),
                (down_in, weights.at[1]),
            )
        )
    ]
    for copy in copies:
        copy.start()
    for copy in copies[:3]:
        copy.wait()
    node_rows, feat_width = key_value.shape[1:]
    ids = lax.broadcasted_iota(jnp.int32, (VIRTUAL, node_rows), 0)
    members = jnp.where(virtual_of[...] == ids, 1.0, 0.0).astype(BF16)
    per_part = sums.shape[1]
    lane_parts = feat_width // LANES
    rows_parts = VIRTUAL // per_part
    for which in range(2):
        pooled = jnp.dot(members, key_value[which], preferred_element_type=F32)
        for row in range(rows_parts):
            for lane in range(lane_parts):
                sums[(which * rows_parts + row) * lane_parts + lane] = pooled[
                    row * per_part : (row + 1) * per_part, lane * LANES : (lane + 1) * LANES
                ]
    for copy in copies[3:]:
        copy.wait()


def plane_sum_kernel(parts, total):
    total[...] = jnp.broadcast_to(jnp.sum(parts[...], axis=0, keepdims=True), total.shape)


def pooled_kernel(scale, parts, after, after_1, after_2, after_3, pooled):
    mean = (jnp.sum(parts[...], axis=0, keepdims=True) * scale).astype(BF16)
    pooled[...] = jnp.broadcast_to(mean, pooled.shape)


def stack_kernel(after, w_0, w_1, w_2, w_3, stacked):
    for i, piece in enumerate((w_0, w_1, w_2, w_3)):
        stacked[i] = piece[...]


def head_pair(queries, block, lanes, low):
    pair = queries[block * BLOCK : (block + 1) * BLOCK, lanes]
    zero = jnp.zeros_like(pair)
    return jnp.concatenate([jnp.where(low, pair, zero), jnp.where(low, zero, pair)], axis=0)


def attend(both, keys, values, ones, bias, scale, low):
    scores = lax.dot_general(both, keys, (((1,), (1,)), ((), ())), preferred_element_type=F32)
    scores = scores * scale
    if bias is not None:
        scores = scores + bias
    row_max = jnp.max(scores, axis=-1, keepdims=True)
    exponent = jnp.exp2(scores - row_max).astype(BF16)
    right = jnp.concatenate([values, ones], axis=1)
    summed = jnp.dot(exponent, right, preferred_element_type=F32)
    top, bottom = summed[:BLOCK], summed[BLOCK:]
    numerator = jnp.where(low, top[:, :LANES], bottom[:, :LANES])
    denominator = jnp.where(low, top[:, LANES:], bottom[:, LANES:])
    return numerator, denominator, jnp.where(low, row_max[:BLOCK], row_max[BLOCK:])


def named(tile_lists, block, place, first_block):
    wanted = first_block + place
    found = tile_lists[block, 0] == wanted
    for slot in range(1, TMAX):
        found = jnp.logical_or(found, tile_lists[block, slot] == wanted)
    return jnp.logical_and(found, wanted >= 0)


def near_kernel(
    tile_lists,
    after,
    queries_in,
    keys,
    values,
    kv_m1,
    kv_p1,
    numerators,
    denominators,
    maxima,
    queries,
    window,
    sem,
):
    rows, feat_width = queries.shape
    head_dim = feat_width // HEADS
    copies = [
        pltpu.make_async_copy(queries_in, queries, sem.at[0]),
        pltpu.make_async_copy(keys, window.at[0, pl.ds(rows, rows)], sem.at[1]),
        pltpu.make_async_copy(values, window.at[1, pl.ds(rows, rows)], sem.at[2]),
        pltpu.make_async_copy(kv_m1, window.at[:, pl.ds(0, rows)], sem.at[3]),
        pltpu.make_async_copy(kv_p1, window.at[:, pl.ds(2 * rows, rows)], sem.at[4]),
    ]
    for copy in copies:
        copy.start()
    for copy in copies:
        copy.wait()
    blocks = rows // BLOCK
    first_block = tile_lists[0, 0] - blocks
    scale = LOG2E / math.sqrt(head_dim)
    low = lax.broadcasted_iota(jnp.int32, (BLOCK, LANES), 1) < head_dim
    for block in range(blocks):
        own = tile_lists[block, 0] - first_block
        starts = []
        shown = []
        for place in range(3 * blocks):
            there = named(tile_lists, block, place, first_block)
            starts.append(pl.multiple_of(jnp.where(there, place, own) * BLOCK, BLOCK))
            shown.append(jnp.full((BLOCK, LANES), jnp.where(there, 1.0, 0.0), F32).astype(BF16))
        for part in range(feat_width // LANES):
            lanes = slice(part * LANES, (part + 1) * LANES)
            keys_here = [window[0, pl.ds(s, BLOCK), lanes] for s in starts]
            values_here = [window[1, pl.ds(s, BLOCK), lanes] * o for s, o in zip(starts, shown)]
            numerator, denominator, row_max = attend(
                head_pair(queries, block, lanes, low),
                jnp.concatenate(keys_here, axis=0),
                jnp.concatenate(values_here, axis=0),
                jnp.concatenate(shown, axis=0),
                None,
                scale,
                low,
            )
            here = slice(block * BLOCK, (block + 1) * BLOCK)
            numerators[here, lanes] = numerator
            denominators[here, lanes] = denominator
            maxima[here, lanes] = row_max


def layer_kernel(
    tile_lists,
    virtual_kv,
    numerators_in,
    denominators_in,
    maxima_in,
    queries_in,
    node_feats_in,
    out_weight_in,
    norm_gain_in,
    kv_m2,
    kv_p2,
    w_near_in,
    partial_out,
    normed_out,
    window,
    numerators,
    denominators,
    maxima,
    queries,
    node_feats,
    out_weight,
    norm_gain,
    w_near,
    attended,
    sem,
):
    rows, feat_width = queries.shape
    copies = [
        pltpu.make_async_copy(source, target, sem.at[i])
        for i, (source, target) in enumerate(
            (
                (queries_in, queries),
                (kv_m2, window.at[:, pl.ds(0, rows)]),
                (kv_p2, window.at[:, pl.ds(rows, rows)]),
                (numerators_in, numerators),
                (denominators_in, denominators),
                (maxima_in, maxima),
                (out_weight_in, out_weight),
                (node_feats_in, node_feats),
                (norm_gain_in, norm_gain),
                (w_near_in, w_near),
            )
        )
    ]
    for copy in copies:
        copy.start()
    for copy in copies[:6]:
        copy.wait()
    head_dim = feat_width // HEADS
    scale = LOG2E / math.sqrt(head_dim)
    lane_parts = feat_width // LANES
    rows_parts = VIRTUAL // virtual_kv.shape[1]
    blocks = rows // BLOCK
    far_blocks = 2 * blocks
    low = lax.broadcasted_iota(jnp.int32, (BLOCK, LANES), 1) < head_dim
    ones = jnp.ones((far_blocks * BLOCK + VIRTUAL, LANES), BF16)
    first_block = tile_lists[0, 0] - 2 * blocks
    for block in range(blocks):
        here = slice(block * BLOCK, (block + 1) * BLOCK)
        bias = [
            jnp.full(
                (1, BLOCK),
                jnp.where(
                    named(tile_lists, block, place + (3 * blocks if place >= blocks else 0), first_block),
                    0.0,
                    -jnp.inf,
                ),
                F32,
            )
            for place in range(far_blocks)
        ]
        bias = jnp.concatenate(bias + [jnp.zeros((1, VIRTUAL), F32)], axis=1)
        for part in range(lane_parts):
            lanes = slice(part * LANES, (part + 1) * LANES)
            pooled = [virtual_kv[r * lane_parts + part] for r in range(2 * rows_parts)]
            numerator, denominator, row_max = attend(
                head_pair(queries, block, lanes, low),
                jnp.concatenate([window[0, :, lanes]] + pooled[:rows_parts], axis=0),
                jnp.concatenate([window[1, :, lanes]] + pooled[rows_parts:], axis=0),
                ones,
                bias,
                scale,
                low,
            )
            near_max = maxima[here, lanes]
            top = jnp.maximum(near_max, row_max)
            keep = jnp.exp2(near_max - top)
            add = jnp.exp2(row_max - top)
            attended[here, lanes] = (
                (numerators[here, lanes] * keep + numerator * add)
                / (denominators[here, lanes] * keep + denominator * add)
            ).astype(BF16)

    for copy in copies[6:9]:
        copy.wait()
    residual = node_feats[...].astype(F32) + jnp.dot(
        attended[...], out_weight[...], preferred_element_type=F32
    )
    row_mean = jnp.mean(residual, axis=-1, keepdims=True)
    centered = residual - row_mean
    variance = jnp.mean(centered * centered, axis=-1, keepdims=True)
    normed = (centered * lax.rsqrt(variance + 1e-05) * norm_gain[...]).astype(BF16)
    normed_out[...] = normed
    copies[9].wait()
    partial_out[...] = residual + hidden_sum(normed, w_near)


def hidden_sum(normed, weights):
    total = 0.0
    for shard in range(weights.shape[0]):
        hidden = jnp.dot(normed, weights[shard, 0], preferred_element_type=F32)
        hidden = jnp.maximum(hidden, 0.0).astype(BF16)
        total = total + lax.dot_general(
            hidden, weights[shard, 1], (((1,), (1,)), ((), ())), preferred_element_type=F32
        )
    return total


def finish_kernel(partial, normed, weights, layer_out):
    layer_out[...] = (partial[...] + hidden_sum(normed[...], weights)).astype(BF16)


def along_dom(shard, by):
    length = lax.axis_size(DOM)
    pairs = [(i, i + by) for i in range(length) if 0 <= i + by < length]
    return lax.ppermute(shard, DOM, pairs)


def around(shard, axis, by):
    length = lax.axis_size(axis)
    return lax.ppermute(shard, axis, [(i, (i + by) % length) for i in range(length)])


def exchanged(parts, axes):
    return lax.all_to_all(parts, axes, 0, 0, tiled=True)


def local(
    node_feats,
    queries,
    keys,
    values,
    out_weight,
    up_weight,
    down_weight,
    norm_gain,
    tile_lists,
    virtual_of,
):
    node_rows, feat_width = queries.shape
    plane = lax.axis_size(PLANE)
    depth = lax.axis_size("z")
    near = lax.axis_size("x")
    per_part = 2 * VIRTUAL * feat_width // LANES // plane
    own_hidden = up_weight.shape[1]
    in_vmem = pl.BlockSpec(memory_space=VMEM)
    in_smem = pl.BlockSpec(memory_space=pltpu.SMEM)
    anywhere = pl.BlockSpec(memory_space=pl.ANY)
    shape = jax.ShapeDtypeStruct

    def grant(mib):
        return pltpu.CompilerParams(vmem_limit_bytes=mib * 1024 * 1024)

    def hbm(array):
        return pltpu.with_memory_space_constraint(array, pltpu.HBM)

    def dma(count):
        return pltpu.SemaphoreType.DMA((count,))

    kv_shape = (2, node_rows, feat_width)
    w_shape = (2, feat_width, own_hidden)
    sums, key_value, w_0 = pl.pallas_call(
        pool_kernel,
        out_shape=(
            shape((plane, per_part, LANES), F32),
            pltpu.HBM(kv_shape, BF16),
            pltpu.HBM(w_shape, BF16),
        ),
        in_specs=[anywhere] * 5,
        out_specs=(in_vmem,) * 3,
        scratch_shapes=[VMEM((1, node_rows), jnp.int32), dma(5)],
        compiler_params=grant(6),
        name="pool",
    )(
        hbm(virtual_of.reshape(1, node_rows)),
        hbm(keys),
        hbm(values),
        hbm(up_weight),
        hbm(down_weight),
    )
    parts = exchanged(sums, PLANE)
    kv_m1 = along_dom(key_value, 1)
    kv_p1 = along_dom(key_value, -1)
    w_1 = around(w_0, "x", 1)
    w_2 = around(w_0, "x", -1)
    w_3 = around(w_0, "x", 2)

    plane_sum = pl.pallas_call(
        plane_sum_kernel,
        out_shape=shape((depth, per_part, LANES), F32),
        in_specs=[in_vmem],
        out_specs=in_vmem,
        compiler_params=grant(2),
        name="plane_sum",
    )(parts)

    parts = exchanged(plane_sum, "z")
    kv_m2 = along_dom(kv_m1, 1)
    kv_p2 = along_dom(kv_p1, -1)
    wide = pltpu.HBM((node_rows, feat_width), F32)
    nears = pl.pallas_call(
        near_kernel,
        out_shape=(wide, wide, wide),
        in_specs=[in_smem] + [anywhere] * 6,
        out_specs=(in_vmem,) * 3,
        scratch_shapes=[
            VMEM((node_rows, feat_width), BF16),
            VMEM((2, 3 * node_rows, feat_width), BF16),
            dma(5),
        ],
        compiler_params=grant(12),
        cost_estimate=pl.CostEstimate(
            flops=4_000_000_000, bytes_accessed=6_000_000, transcendentals=2_000_000
        ),
        name="near",
    )(tile_lists, plane_sum, hbm(queries), hbm(keys), hbm(values), kv_m1, kv_p1)

    pool_scale = math.sqrt(VIRTUAL / (node_rows * lax.axis_size(AXES)))
    pooled = pl.pallas_call(
        functools.partial(pooled_kernel, pool_scale),
        out_shape=shape((plane, per_part, LANES), BF16),
        in_specs=[in_vmem] + [anywhere] * 4,
        out_specs=in_vmem,
        compiler_params=grant(2),
        name="pooled",
    )(parts, hbm(nears[2]), w_1, w_2, w_3)

    virtual_kv = exchanged(pooled, PLANE)
    w_near = pl.pallas_call(
        stack_kernel,
        out_shape=pltpu.HBM((near, *w_shape), BF16),
        in_specs=[anywhere] + [in_vmem] * near,
        out_specs=in_vmem,
        compiler_params=grant(6),
        name="stack",
    )(pooled, hbm(w_0), w_1, w_2, w_3)
    w_far = around(w_near, "c", 1)

    partial, normed = pl.pallas_call(
        layer_kernel,
        out_shape=(wide, shape((node_rows, feat_width), BF16)),
        in_specs=[in_smem, in_vmem] + [anywhere] * 10,
        out_specs=(in_vmem,) * 2,
        scratch_shapes=[
            VMEM((2, 2 * node_rows, feat_width), BF16),
            VMEM((node_rows, feat_width), F32),
            VMEM((node_rows, feat_width), F32),
            VMEM((node_rows, feat_width), F32),
            VMEM((node_rows, feat_width), BF16),
            VMEM((node_rows, feat_width), BF16),
            VMEM(out_weight.shape, BF16),
            VMEM((1, feat_width), F32),
            VMEM((near, *w_shape), BF16),
            VMEM((node_rows, feat_width), BF16),
            dma(10),
        ],
        compiler_params=grant(20),
        cost_estimate=pl.CostEstimate(
            flops=400_000_000_000, bytes_accessed=6_000_000, transcendentals=2_000_000
        ),
        name="layer",
    )(
        tile_lists,
        virtual_kv,
        *[hbm(part) for part in nears],
        hbm(queries),
        hbm(node_feats),
        hbm(out_weight),
        hbm(norm_gain.reshape(1, feat_width)),
        kv_m2,
        kv_p2,
        hbm(w_near),
    )
    return pl.pallas_call(
        finish_kernel,
        out_shape=shape((node_rows, feat_width), BF16),
        in_specs=[in_vmem] * 3,
        out_specs=in_vmem,
        compiler_params=grant(10),
        name="finish",
    )(hbm(partial), normed, w_far)


def solution(mesh):
    group, dom = mesh.devices.shape
    fine = Mesh(mesh.devices.reshape(group // 2, 2, dom // 4, 4), AXES)
    placed = (
        P(AXES, None),
        P(AXES, None),
        P(AXES, None),
        P(AXES, None),
        P(),
        P(None, ("x", "c")),
        P(None, ("x", "c")),
        P(),
        P(AXES, None),
        P(AXES),
    )
    return jax.shard_map(
        local, mesh=fine, in_specs=placed, out_specs=P(AXES, None), check_vma=False
    )
```

```python
import functools
import math

import jax
import jax.numpy as jnp
from jax import lax
from jax.experimental import pallas as pl
from jax.experimental.pallas import tpu as pltpu
from jax.sharding import Mesh
from jax.sharding import PartitionSpec as P

HEADS = 8
BLOCK = 128
VIRTUAL = 64
REACH = 2
TMAX = 6
LANES = 128
LOG2E = 1.4426950408889634
AXES = ("x", "c", "z", "y")
DOM = ("z", "y")
PLANE = ("x", "c", "y")
VMEM = pltpu.VMEM
F32 = jnp.float32
BF16 = jnp.bfloat16


def pool_kernel(
    virtual_of_in, keys_in, values_in, up_in, down_in, sums, key_value, weights, virtual_of, sem
):
    copies = [
        pltpu.make_async_copy(source, target, sem.at[i])
        for i, (source, target) in enumerate(
            (
                (virtual_of_in, virtual_of),
                (keys_in, key_value.at[0]),
                (values_in, key_value.at[1]),
                (up_in, weights.at[0]),
                (down_in, weights.at[1]),
            )
        )
    ]
    for copy in copies:
        copy.start()
    for copy in copies[:3]:
        copy.wait()
    node_rows, feat_width = key_value.shape[1:]
    ids = lax.broadcasted_iota(jnp.int32, (VIRTUAL, node_rows), 0)
    members = jnp.where(virtual_of[...] == ids, 1.0, 0.0).astype(BF16)
    per_part = sums.shape[1]
    lane_parts = feat_width // LANES
    rows_parts = VIRTUAL // per_part
    for which in range(2):
        pooled = jnp.dot(members, key_value[which], preferred_element_type=F32)
        for row in range(rows_parts):
            for lane in range(lane_parts):
                sums[(which * rows_parts + row) * lane_parts + lane] = pooled[
                    row * per_part : (row + 1) * per_part, lane * LANES : (lane + 1) * LANES
                ]
    for copy in copies[3:]:
        copy.wait()


def plane_sum_kernel(parts, total):
    total[...] = jnp.broadcast_to(jnp.sum(parts[...], axis=0, keepdims=True), total.shape)


def pooled_kernel(scale, parts, after, after_1, after_2, pooled):
    mean = (jnp.sum(parts[...], axis=0, keepdims=True) * scale).astype(BF16)
    pooled[...] = jnp.broadcast_to(mean, pooled.shape)


def stack_kernel(after, w_0, w_1, w_2, w_3, stacked):
    for i, piece in enumerate((w_0, w_1, w_2, w_3)):
        stacked[i] = piece[...]


def named(tile_lists, block, wanted):
    found = tile_lists[block, 0] == wanted
    for slot in range(1, TMAX):
        found = jnp.logical_or(found, tile_lists[block, slot] == wanted)
    return jnp.logical_and(found, wanted >= 0)


def gate_kernel(after, left, right, token):
    token[...] = jnp.zeros_like(token)


def layer_kernel(
    tile_lists,
    virtual_kv,
    queries_in,
    keys,
    values,
    kv_m1,
    kv_p1,
    kv_m2,
    kv_p2,
    out_weight_in,
    node_feats_in,
    norm_gain_in,
    w_near_in,
    partial_out,
    normed_out,
    queries,
    window,
    out_weight,
    node_feats,
    norm_gain,
    w_near,
    attended,
    sem,
):
    rows, feat_width = queries.shape
    near = w_near.shape[0]
    middle = REACH * rows
    moves = [
        (queries_in, queries),
        (keys, window.at[0, pl.ds(middle, rows)]),
        (values, window.at[1, pl.ds(middle, rows)]),
        (kv_m1, window.at[:, pl.ds(rows, rows)]),
        (kv_p1, window.at[:, pl.ds(3 * rows, rows)]),
        (kv_m2, window.at[:, pl.ds(0, rows)]),
        (kv_p2, window.at[:, pl.ds(4 * rows, rows)]),
        (out_weight_in, out_weight),
        (node_feats_in, node_feats),
        (norm_gain_in, norm_gain),
    ]
    moves += [(w_near_in.at[shard], w_near.at[shard]) for shard in range(near)]
    copies = [
        pltpu.make_async_copy(source, target, sem.at[i])
        for i, (source, target) in enumerate(moves)
    ]
    for copy in copies:
        copy.start()
    head_dim = feat_width // HEADS
    scale = LOG2E / math.sqrt(head_dim)
    lane_parts = feat_width // LANES
    rows_parts = VIRTUAL // virtual_kv.shape[1]
    blocks = rows // BLOCK
    places = (2 * REACH + 1) * blocks
    low = lax.broadcasted_iota(jnp.int32, (BLOCK, LANES), 1) < head_dim
    ones = jnp.ones((places * BLOCK + VIRTUAL, LANES), BF16)
    first_block = tile_lists[0, 0] - REACH * blocks
    bias = [
        jnp.concatenate(
            [
                jnp.full(
                    (1, BLOCK),
                    jnp.where(named(tile_lists, block, first_block + place), 0.0, -jnp.inf),
                    F32,
                )
                for place in range(places)
            ]
            + [jnp.zeros((1, VIRTUAL), F32)],
            axis=1,
        )
        for block in range(blocks)
    ]
    for copy in copies[:7]:
        copy.wait()
    for part in range(lane_parts):
        lanes = slice(part * LANES, (part + 1) * LANES)
        pooled = [virtual_kv[r * lane_parts + part] for r in range(2 * rows_parts)]
        all_keys = jnp.concatenate([window[0, :, lanes]] + pooled[:rows_parts], axis=0)
        all_values = jnp.concatenate([window[1, :, lanes]] + pooled[rows_parts:], axis=0)
        right = jnp.concatenate([all_values, ones], axis=1)
        for block in range(blocks):
            here = slice(block * BLOCK, (block + 1) * BLOCK)
            pair = queries[here, lanes]
            zero = jnp.zeros_like(pair)
            both = jnp.concatenate(
                [jnp.where(low, pair, zero), jnp.where(low, zero, pair)], axis=0
            )
            scores = lax.dot_general(
                both, all_keys, (((1,), (1,)), ((), ())), preferred_element_type=F32
            )
            scores = scores * scale + bias[block]
            row_max = jnp.max(scores, axis=-1, keepdims=True)
            exponent = jnp.exp2(scores - row_max).astype(BF16)
            summed = jnp.dot(exponent, right, preferred_element_type=F32)
            result = summed[:, :LANES] / summed[:, LANES:]
            attended[here, lanes] = jnp.where(low, result[:BLOCK], result[BLOCK:]).astype(BF16)

    for copy in copies[7:10]:
        copy.wait()
    residual = node_feats[...].astype(F32) + jnp.dot(
        attended[...], out_weight[...], preferred_element_type=F32
    )
    row_mean = jnp.mean(residual, axis=-1, keepdims=True)
    centered = residual - row_mean
    variance = jnp.mean(centered * centered, axis=-1, keepdims=True)
    normed = (centered * lax.rsqrt(variance + 1e-05) * norm_gain[...]).astype(BF16)
    normed_out[...] = normed
    partial_out[...] = residual + hidden_sum(normed, w_near, copies[10:])


def hidden_sum(normed, weights, copies):
    total = 0.0
    for shard, copy in enumerate(copies):
        copy.wait()
        hidden = jnp.dot(normed, weights[shard, 0], preferred_element_type=F32)
        hidden = jnp.maximum(hidden, 0.0).astype(BF16)
        total = total + lax.dot_general(
            hidden, weights[shard, 1], (((1,), (1,)), ((), ())), preferred_element_type=F32
        )
    return total


def finish_kernel(partial, normed, weights_in, layer_out, weights, sem):
    copies = [
        pltpu.make_async_copy(weights_in.at[shard], weights.at[shard], sem.at[shard])
        for shard in range(weights.shape[0])
    ]
    for copy in copies:
        copy.start()
    layer_out[...] = (partial[...] + hidden_sum(normed[...], weights, copies)).astype(BF16)


def along_dom(shard, by):
    length = lax.axis_size(DOM)
    pairs = [(i, i + by) for i in range(length) if 0 <= i + by < length]
    return lax.ppermute(shard, DOM, pairs)


def around(shard, axis, by):
    length = lax.axis_size(axis)
    return lax.ppermute(shard, axis, [(i, (i + by) % length) for i in range(length)])


def exchanged(parts, axes):
    return lax.all_to_all(parts, axes, 0, 0, tiled=True)


def local(
    node_feats,
    queries,
    keys,
    values,
    out_weight,
    up_weight,
    down_weight,
    norm_gain,
    tile_lists,
    virtual_of,
):
    node_rows, feat_width = queries.shape
    plane = lax.axis_size(PLANE)
    depth = lax.axis_size("z")
    near = lax.axis_size("x")
    per_part = 2 * VIRTUAL * feat_width // LANES // plane
    own_hidden = up_weight.shape[1]
    in_vmem = pl.BlockSpec(memory_space=VMEM)
    in_smem = pl.BlockSpec(memory_space=pltpu.SMEM)
    anywhere = pl.BlockSpec(memory_space=pl.ANY)
    shape = jax.ShapeDtypeStruct

    def grant(mib):
        return pltpu.CompilerParams(vmem_limit_bytes=mib * 1024 * 1024)

    def hbm(array):
        return pltpu.with_memory_space_constraint(array, pltpu.HBM)

    def vmem(array):
        return pltpu.with_memory_space_constraint(array, VMEM)

    def dma(count):
        return pltpu.SemaphoreType.DMA((count,))

    kv_shape = (2, node_rows, feat_width)
    w_shape = (2, feat_width, own_hidden)
    sums, key_value, w_0 = pl.pallas_call(
        pool_kernel,
        out_shape=(
            shape((plane, per_part, LANES), F32),
            pltpu.HBM(kv_shape, BF16),
            pltpu.HBM(w_shape, BF16),
        ),
        in_specs=[anywhere] * 5,
        out_specs=(in_vmem,) * 3,
        scratch_shapes=[VMEM((1, node_rows), jnp.int32), dma(5)],
        compiler_params=grant(6),
        name="pool",
    )(
        hbm(virtual_of.reshape(1, node_rows)),
        hbm(keys),
        hbm(values),
        hbm(up_weight),
        hbm(down_weight),
    )
    parts = exchanged(sums, PLANE)
    kv_m1 = along_dom(key_value, 1)
    kv_p1 = along_dom(key_value, -1)
    w_1 = around(w_0, "x", 1)
    w_2 = around(w_0, "x", -1)
    w_3 = around(w_0, "x", 2)

    plane_sum = pl.pallas_call(
        plane_sum_kernel,
        out_shape=shape((depth, per_part, LANES), F32),
        in_specs=[in_vmem],
        out_specs=in_vmem,
        compiler_params=grant(2),
        cost_estimate=pl.CostEstimate(
            flops=8_000_000_000, bytes_accessed=400_000, transcendentals=0
        ),
        name="plane_sum",
    )(parts)

    parts = exchanged(plane_sum, "z")
    kv_m2 = along_dom(kv_m1, 1)
    kv_p2 = along_dom(kv_p1, -1)
    token = pl.pallas_call(
        gate_kernel,
        out_shape=pltpu.HBM((8, LANES), F32),
        in_specs=[anywhere] * 3,
        out_specs=in_vmem,
        compiler_params=grant(2),
        cost_estimate=pl.CostEstimate(
            flops=4_000_000_000, bytes_accessed=6_000_000, transcendentals=2_000_000
        ),
        name="gate",
    )(plane_sum, kv_m1, kv_p1)

    pool_scale = math.sqrt(VIRTUAL / (node_rows * lax.axis_size(AXES)))
    pooled = pl.pallas_call(
        functools.partial(pooled_kernel, pool_scale),
        out_shape=shape((plane, per_part, LANES), BF16),
        in_specs=[in_vmem] + [anywhere] * 3,
        out_specs=in_vmem,
        compiler_params=grant(2),
        name="pooled",
    )(parts, hbm(token), w_1, w_2)

    virtual_kv = exchanged(pooled, PLANE)
    w_near = pl.pallas_call(
        stack_kernel,
        out_shape=pltpu.HBM((near, *w_shape), BF16),
        in_specs=[anywhere] + [in_vmem] * near,
        out_specs=in_vmem,
        compiler_params=grant(6),
        name="stack",
    )(pooled, hbm(w_0), w_1, w_2, w_3)
    w_far = around(w_near, "c", 1)

    partial, normed = pl.pallas_call(
        layer_kernel,
        out_shape=(VMEM((node_rows, feat_width), F32), VMEM((node_rows, feat_width), BF16)),
        in_specs=[in_smem, in_vmem] + [anywhere] * 11,
        out_specs=(in_vmem,) * 2,
        scratch_shapes=[
            VMEM((node_rows, feat_width), BF16),
            VMEM((2, (2 * REACH + 1) * node_rows, feat_width), BF16),
            VMEM(out_weight.shape, BF16),
            VMEM((node_rows, feat_width), BF16),
            VMEM((1, feat_width), F32),
            VMEM((near, *w_shape), BF16),
            VMEM((node_rows, feat_width), BF16),
            dma(10 + near),
        ],
        compiler_params=grant(20),
        cost_estimate=pl.CostEstimate(
            flops=400_000_000_000, bytes_accessed=6_000_000, transcendentals=2_000_000
        ),
        name="layer",
    )(
        tile_lists,
        virtual_kv,
        hbm(queries),
        hbm(keys),
        hbm(values),
        kv_m1,
        kv_p1,
        kv_m2,
        kv_p2,
        hbm(out_weight),
        hbm(node_feats),
        hbm(norm_gain.reshape(1, feat_width)),
        hbm(w_near),
    )
    return pl.pallas_call(
        finish_kernel,
        out_shape=shape((node_rows, feat_width), BF16),
        in_specs=[in_vmem, in_vmem, anywhere],
        out_specs=in_vmem,
        scratch_shapes=[VMEM((near, *w_shape), BF16), dma(near)],
        compiler_params=grant(10),
        name="finish",
    )(vmem(partial), vmem(normed), w_far)


def solution(mesh):
    group, dom = mesh.devices.shape
    fine = Mesh(mesh.devices.reshape(group // 2, 2, dom // 4, 4), AXES)
    placed = (
        P(AXES, None),
        P(AXES, None),
        P(AXES, None),
        P(AXES, None),
        P(),
        P(None, ("x", "c")),
        P(None, ("x", "c")),
        P(),
        P(AXES, None),
        P(AXES),
    )
    return jax.shard_map(
        local, mesh=fine, in_specs=placed, out_specs=P(AXES, None), check_vma=False
    )
```

```python
import functools
import math

import jax
import jax.numpy as jnp
from jax import lax
from jax.experimental import pallas as pl
from jax.experimental.pallas import tpu as pltpu
from jax.sharding import Mesh
from jax.sharding import PartitionSpec as P

HEADS = 8
BLOCK = 128
VIRTUAL = 64
REACH = 2
TMAX = 6
LANES = 128
LOG2E = 1.4426950408889634
AXES = ("x", "c", "z", "y")
DOM = ("z", "y")
PLANE = ("x", "c", "y")
VMEM = pltpu.VMEM
F32 = jnp.float32
BF16 = jnp.bfloat16


def pool_kernel(
    virtual_of_in, keys_in, values_in, up_in, down_in, sums, key_value, weights, virtual_of, sem
):
    copies = [
        pltpu.make_async_copy(source, target, sem.at[i])
        for i, (source, target) in enumerate(
            (
                (virtual_of_in, virtual_of),
                (keys_in, key_value.at[0]),
                (values_in, key_value.at[1]),
                (up_in, weights.at[0]),
                (down_in, weights.at[1]),
            )
        )
    ]
    for copy in copies:
        copy.start()
    for copy in copies[:3]:
        copy.wait()
    node_rows, feat_width = key_value.shape[1:]
    ids = lax.broadcasted_iota(jnp.int32, (VIRTUAL, node_rows), 0)
    members = jnp.where(virtual_of[...] == ids, 1.0, 0.0).astype(BF16)
    per_part = sums.shape[1]
    lane_parts = feat_width // LANES
    rows_parts = VIRTUAL // per_part
    for which in range(2):
        pooled = jnp.dot(members, key_value[which], preferred_element_type=F32)
        for row in range(rows_parts):
            for lane in range(lane_parts):
                sums[(which * rows_parts + row) * lane_parts + lane] = pooled[
                    row * per_part : (row + 1) * per_part, lane * LANES : (lane + 1) * LANES
                ]
    for copy in copies[3:]:
        copy.wait()


def plane_sum_kernel(parts, total):
    total[...] = jnp.broadcast_to(jnp.sum(parts[...], axis=0, keepdims=True), total.shape)


def pooled_kernel(scale, parts, after, after_1, pooled):
    mean = (jnp.sum(parts[...], axis=0, keepdims=True) * scale).astype(BF16)
    pooled[...] = jnp.broadcast_to(mean, pooled.shape)


def named(tile_lists, block, wanted):
    found = tile_lists[block, 0] == wanted
    for slot in range(1, TMAX):
        found = jnp.logical_or(found, tile_lists[block, slot] == wanted)
    return jnp.logical_and(found, wanted >= 0)


def stack_kernel(tile_lists, after, w_0, w_1, w_2, w_3, stacked, bias):
    for i, piece in enumerate((w_0, w_1, w_2, w_3)):
        stacked[i] = piece[...]
    blocks, width = bias.shape
    first_block = tile_lists[0, 0] - REACH * blocks
    for block in range(blocks):
        for place in range((2 * REACH + 1) * blocks):
            here = pl.ds(place * BLOCK, BLOCK)
            there = named(tile_lists, block, first_block + place)
            bias[pl.ds(block, 1), here] = jnp.full((1, BLOCK), jnp.where(there, 0.0, -jnp.inf), F32)
        bias[pl.ds(block, 1), pl.ds(width - VIRTUAL, VIRTUAL)] = jnp.zeros((1, VIRTUAL), F32)


def gate_kernel(after, left, right, token):
    token[...] = jnp.zeros_like(token)


def layer_kernel(
    virtual_kv,
    kv_m1,
    kv_p1,
    kv_p2,
    kv_m2,
    queries_in,
    keys,
    values,
    bias_in,
    out_weight_in,
    node_feats_in,
    norm_gain_in,
    w_near_in,
    partial_out,
    normed_out,
    queries,
    own,
    left,
    bias,
    out_weight,
    node_feats,
    norm_gain,
    w_near,
    attended,
    sem,
):
    rows, feat_width = queries.shape
    near = w_near.shape[0]
    moves = [
        (queries_in, queries),
        (keys, own.at[0]),
        (values, own.at[1]),
        (kv_m2, left),
        (bias_in, bias),
        (out_weight_in, out_weight),
        (node_feats_in, node_feats),
        (norm_gain_in, norm_gain),
    ]
    moves += [(w_near_in.at[shard], w_near.at[shard]) for shard in range(near)]
    copies = [
        pltpu.make_async_copy(source, target, sem.at[i])
        for i, (source, target) in enumerate(moves)
    ]
    for copy in copies:
        copy.start()
    head_dim = feat_width // HEADS
    scale = LOG2E / math.sqrt(head_dim)
    lane_parts = feat_width // LANES
    rows_parts = VIRTUAL // virtual_kv.shape[1]
    blocks = rows // BLOCK
    low = lax.broadcasted_iota(jnp.int32, (BLOCK, LANES), 1) < head_dim
    ones = jnp.ones((bias.shape[1], LANES), BF16)
    for copy in copies[:5]:
        copy.wait()
    pieces = (left, kv_m1, own, kv_p1, kv_p2)
    for part in range(lane_parts):
        lanes = slice(part * LANES, (part + 1) * LANES)
        pooled = [virtual_kv[r * lane_parts + part] for r in range(2 * rows_parts)]
        all_keys = jnp.concatenate(
            [piece[0, :, lanes] for piece in pieces] + pooled[:rows_parts], axis=0
        )
        all_values = jnp.concatenate(
            [piece[1, :, lanes] for piece in pieces] + pooled[rows_parts:], axis=0
        )
        right = jnp.concatenate([all_values, ones], axis=1)
        for block in range(blocks):
            here = slice(block * BLOCK, (block + 1) * BLOCK)
            pair = queries[here, lanes]
            zero = jnp.zeros_like(pair)
            both = jnp.concatenate(
                [jnp.where(low, pair, zero), jnp.where(low, zero, pair)], axis=0
            )
            scores = lax.dot_general(
                both, all_keys, (((1,), (1,)), ((), ())), preferred_element_type=F32
            )
            scores = scores * scale + bias[pl.ds(block, 1), :]
            row_max = jnp.max(scores, axis=-1, keepdims=True)
            exponent = jnp.exp2(scores - row_max).astype(BF16)
            summed = jnp.dot(exponent, right, preferred_element_type=F32)
            result = summed[:, :LANES] / summed[:, LANES:]
            attended[here, lanes] = jnp.where(low, result[:BLOCK], result[BLOCK:]).astype(BF16)

    for copy in copies[5:8]:
        copy.wait()
    residual = node_feats[...].astype(F32) + jnp.dot(
        attended[...], out_weight[...], preferred_element_type=F32
    )
    row_mean = jnp.mean(residual, axis=-1, keepdims=True)
    centered = residual - row_mean
    variance = jnp.mean(centered * centered, axis=-1, keepdims=True)
    normed = (centered * lax.rsqrt(variance + 1e-05) * norm_gain[...]).astype(BF16)
    normed_out[...] = normed
    partial_out[...] = residual + hidden_sum(normed, w_near, copies[8:])


def hidden_sum(normed, weights, copies):
    total = 0.0
    for shard, copy in enumerate(copies):
        copy.wait()
        hidden = jnp.dot(normed, weights[shard, 0], preferred_element_type=F32)
        hidden = jnp.maximum(hidden, 0.0).astype(BF16)
        total = total + lax.dot_general(
            hidden, weights[shard, 1], (((1,), (1,)), ((), ())), preferred_element_type=F32
        )
    return total


def finish_kernel(partial, normed, weights_in, layer_out, weights, sem):
    copies = [
        pltpu.make_async_copy(weights_in.at[shard], weights.at[shard], sem.at[shard])
        for shard in range(weights.shape[0])
    ]
    for copy in copies:
        copy.start()
    layer_out[...] = (partial[...] + hidden_sum(normed[...], weights, copies)).astype(BF16)


def along_dom(shard, by):
    length = lax.axis_size(DOM)
    pairs = [(i, i + by) for i in range(length) if 0 <= i + by < length]
    return lax.ppermute(shard, DOM, pairs)


def around(shard, axis, by):
    length = lax.axis_size(axis)
    return lax.ppermute(shard, axis, [(i, (i + by) % length) for i in range(length)])


def exchanged(parts, axes):
    return lax.all_to_all(parts, axes, 0, 0, tiled=True)


def local(
    node_feats,
    queries,
    keys,
    values,
    out_weight,
    up_weight,
    down_weight,
    norm_gain,
    tile_lists,
    virtual_of,
):
    node_rows, feat_width = queries.shape
    plane = lax.axis_size(PLANE)
    depth = lax.axis_size("z")
    near = lax.axis_size("x")
    blocks = node_rows // BLOCK
    per_part = 2 * VIRTUAL * feat_width // LANES // plane
    own_hidden = up_weight.shape[1]
    in_vmem = pl.BlockSpec(memory_space=VMEM)
    in_smem = pl.BlockSpec(memory_space=pltpu.SMEM)
    anywhere = pl.BlockSpec(memory_space=pl.ANY)
    shape = jax.ShapeDtypeStruct

    def grant(mib):
        return pltpu.CompilerParams(vmem_limit_bytes=mib * 1024 * 1024)

    def hbm(array):
        return pltpu.with_memory_space_constraint(array, pltpu.HBM)

    def vmem(array):
        return pltpu.with_memory_space_constraint(array, VMEM)

    def dma(count):
        return pltpu.SemaphoreType.DMA((count,))

    kv_shape = (2, node_rows, feat_width)
    w_shape = (2, feat_width, own_hidden)
    sums, key_value, w_0 = pl.pallas_call(
        pool_kernel,
        out_shape=(
            shape((plane, per_part, LANES), F32),
            pltpu.HBM(kv_shape, BF16),
            pltpu.HBM(w_shape, BF16),
        ),
        in_specs=[anywhere] * 5,
        out_specs=(in_vmem,) * 3,
        scratch_shapes=[VMEM((1, node_rows), jnp.int32), dma(5)],
        compiler_params=grant(6),
        name="pool",
    )(
        hbm(virtual_of.reshape(1, node_rows)),
        hbm(keys),
        hbm(values),
        hbm(up_weight),
        hbm(down_weight),
    )
    parts = exchanged(sums, PLANE)
    kv_m1 = along_dom(key_value, 1)
    kv_p1 = along_dom(key_value, -1)
    w_1 = around(w_0, "x", 1)
    w_2 = around(w_0, "x", -1)
    w_3 = around(w_0, "x", 2)

    plane_sum = pl.pallas_call(
        plane_sum_kernel,
        out_shape=shape((depth, per_part, LANES), F32),
        in_specs=[in_vmem],
        out_specs=in_vmem,
        compiler_params=grant(2),
        cost_estimate=pl.CostEstimate(
            flops=8_000_000_000, bytes_accessed=400_000, transcendentals=0
        ),
        name="plane_sum",
    )(parts)

    parts = exchanged(plane_sum, "z")
    kv_m2 = along_dom(kv_m1, 1)
    kv_p2 = along_dom(kv_p1, -1)
    token = pl.pallas_call(
        gate_kernel,
        out_shape=pltpu.HBM((8, LANES), F32),
        in_specs=[anywhere] * 3,
        out_specs=in_vmem,
        compiler_params=grant(2),
        cost_estimate=pl.CostEstimate(
            flops=4_000_000_000, bytes_accessed=6_000_000, transcendentals=2_000_000
        ),
        name="gate",
    )(plane_sum, kv_m1, kv_p1)

    pool_scale = math.sqrt(VIRTUAL / (node_rows * lax.axis_size(AXES)))
    pooled = pl.pallas_call(
        functools.partial(pooled_kernel, pool_scale),
        out_shape=shape((plane, per_part, LANES), BF16),
        in_specs=[in_vmem] + [anywhere] * 2,
        out_specs=in_vmem,
        compiler_params=grant(2),
        name="pooled",
    )(parts, hbm(token), w_3)

    virtual_kv = exchanged(pooled, PLANE)
    w_near, bias = pl.pallas_call(
        stack_kernel,
        out_shape=(
            pltpu.HBM((near, *w_shape), BF16),
            pltpu.HBM((blocks, (2 * REACH + 1) * node_rows + VIRTUAL), F32),
        ),
        in_specs=[in_smem, anywhere] + [in_vmem] * near,
        out_specs=(in_vmem,) * 2,
        compiler_params=grant(6),
        name="stack",
    )(tile_lists, pooled, hbm(w_0), w_1, w_2, w_3)
    w_far = around(w_near, "c", 1)

    partial, normed = pl.pallas_call(
        layer_kernel,
        out_shape=(VMEM((node_rows, feat_width), F32), VMEM((node_rows, feat_width), BF16)),
        in_specs=[in_vmem] * 4 + [anywhere] * 9,
        out_specs=(in_vmem,) * 2,
        scratch_shapes=[
            VMEM((node_rows, feat_width), BF16),
            VMEM(kv_shape, BF16),
            VMEM(kv_shape, BF16),
            VMEM(bias.shape, F32),
            VMEM(out_weight.shape, BF16),
            VMEM((node_rows, feat_width), BF16),
            VMEM((1, feat_width), F32),
            VMEM((near, *w_shape), BF16),
            VMEM((node_rows, feat_width), BF16),
            dma(8 + near),
        ],
        compiler_params=grant(20),
        cost_estimate=pl.CostEstimate(
            flops=400_000_000_000, bytes_accessed=6_000_000, transcendentals=2_000_000
        ),
        name="layer",
    )(
        virtual_kv,
        kv_m1,
        kv_p1,
        kv_p2,
        kv_m2,
        hbm(queries),
        hbm(keys),
        hbm(values),
        hbm(bias),
        hbm(out_weight),
        hbm(node_feats),
        hbm(norm_gain.reshape(1, feat_width)),
        hbm(w_near),
    )
    return pl.pallas_call(
        finish_kernel,
        out_shape=shape((node_rows, feat_width), BF16),
        in_specs=[in_vmem, in_vmem, anywhere],
        out_specs=in_vmem,
        scratch_shapes=[VMEM((near, *w_shape), BF16), dma(near)],
        compiler_params=grant(10),
        name="finish",
    )(vmem(partial), vmem(normed), w_far)


def solution(mesh):
    group, dom = mesh.devices.shape
    fine = Mesh(mesh.devices.reshape(group // 2, 2, dom // 4, 4), AXES)
    placed = (
        P(AXES, None),
        P(AXES, None),
        P(AXES, None),
        P(AXES, None),
        P(),
        P(None, ("x", "c")),
        P(None, ("x", "c")),
        P(),
        P(AXES, None),
        P(AXES),
    )
    return jax.shard_map(
        local, mesh=fine, in_specs=placed, out_specs=P(AXES, None), check_vma=False
    )
```

```python
import functools
import math

import jax
import jax.numpy as jnp
from jax import lax
from jax.experimental import pallas as pl
from jax.experimental.pallas import tpu as pltpu
from jax.sharding import Mesh
from jax.sharding import PartitionSpec as P

HEADS = 8
BLOCK = 128
VIRTUAL = 64
REACH = 2
TMAX = 6
LANES = 128
LOG2E = 1.4426950408889634
AXES = ("x", "c", "z", "y")
DOM = ("z", "y")
PLANE = ("x", "c", "y")
VMEM = pltpu.VMEM
F32 = jnp.float32
BF16 = jnp.bfloat16


def pool_kernel(
    virtual_of_in, keys_in, values_in, up_in, down_in, sums, key_value, weights, virtual_of, sem
):
    copies = [
        pltpu.make_async_copy(source, target, sem.at[i])
        for i, (source, target) in enumerate(
            (
                (virtual_of_in, virtual_of),
                (keys_in, key_value.at[0]),
                (values_in, key_value.at[1]),
                (up_in, weights.at[0]),
                (down_in, weights.at[1]),
            )
        )
    ]
    for copy in copies:
        copy.start()
    for copy in copies[:3]:
        copy.wait()
    node_rows, feat_width = key_value.shape[1:]
    ids = lax.broadcasted_iota(jnp.int32, (VIRTUAL, node_rows), 0)
    members = jnp.where(virtual_of[...] == ids, 1.0, 0.0).astype(BF16)
    per_part = sums.shape[1]
    lane_parts = feat_width // LANES
    rows_parts = VIRTUAL // per_part
    for which in range(2):
        pooled = jnp.dot(members, key_value[which], preferred_element_type=F32)
        for row in range(rows_parts):
            for lane in range(lane_parts):
                sums[(which * rows_parts + row) * lane_parts + lane] = pooled[
                    row * per_part : (row + 1) * per_part, lane * LANES : (lane + 1) * LANES
                ]
    for copy in copies[3:]:
        copy.wait()


def plane_sum_kernel(parts, total):
    total[...] = jnp.broadcast_to(jnp.sum(parts[...], axis=0, keepdims=True), total.shape)


def pooled_kernel(scale, parts, after, after_1, pooled):
    mean = (jnp.sum(parts[...], axis=0, keepdims=True) * scale).astype(BF16)
    pooled[...] = jnp.broadcast_to(mean, pooled.shape)


def stack_kernel(after, w_0, w_1, w_2, w_3, stacked):
    for i, piece in enumerate((w_0, w_1, w_2, w_3)):
        stacked[i] = piece[...]


def gate_kernel(after, left, right, token):
    token[...] = jnp.zeros_like(token)


def layer_kernel(
    tile_lists,
    virtual_kv,
    queries_in,
    keys,
    values,
    kv_m1,
    kv_p1,
    kv_p2,
    kv_m2,
    out_weight_in,
    node_feats_in,
    norm_gain_in,
    w_near_in,
    partial_out,
    normed_out,
    queries,
    window,
    out_weight,
    node_feats,
    norm_gain,
    w_near,
    attended,
    sem,
):
    rows, feat_width = queries.shape
    near = w_near.shape[0]
    middle = REACH * rows
    moves = [
        (queries_in, queries),
        (keys, window.at[0, pl.ds(middle, rows)]),
        (values, window.at[1, pl.ds(middle, rows)]),
        (kv_m2, window.at[:, pl.ds(0, rows)]),
        (kv_p2, window.at[:, pl.ds(4 * rows, rows)]),
        (kv_m1, window.at[:, pl.ds(rows, rows)]),
        (kv_p1, window.at[:, pl.ds(3 * rows, rows)]),
        (out_weight_in, out_weight),
        (node_feats_in, node_feats),
        (norm_gain_in, norm_gain),
    ]
    moves += [(w_near_in.at[shard], w_near.at[shard]) for shard in range(near)]
    copies = [
        pltpu.make_async_copy(source, target, sem.at[i])
        for i, (source, target) in enumerate(moves)
    ]
    for copy in copies:
        copy.start()
    head_dim = feat_width // HEADS
    scale = LOG2E / math.sqrt(head_dim)
    lane_parts = feat_width // LANES
    rows_parts = VIRTUAL // virtual_kv.shape[1]
    blocks = rows // BLOCK
    low = lax.broadcasted_iota(jnp.int32, (BLOCK, LANES), 1) < head_dim
    first_block = tile_lists[0, 0] - REACH * blocks
    starts = []
    shown = []
    for block in range(blocks):
        own = tile_lists[block, 0]
        for slot in range(TMAX):
            tile = tile_lists[block, slot]
            there = tile >= 0
            place = jnp.where(there, tile, own) - first_block
            starts.append(pl.multiple_of(place * BLOCK, BLOCK))
            shown.append(jnp.full((BLOCK, LANES), jnp.where(there, 1.0, 0.0), F32).astype(BF16))
    for copy in copies[:7]:
        copy.wait()
    for part in range(lane_parts):
        lanes = slice(part * LANES, (part + 1) * LANES)
        pooled = [virtual_kv[r * lane_parts + part] for r in range(2 * rows_parts)]
        for block in range(blocks):
            slots = range(block * TMAX, (block + 1) * TMAX)
            here = slice(block * BLOCK, (block + 1) * BLOCK)
            pair = queries[here, lanes]
            zero = jnp.zeros_like(pair)
            both = jnp.concatenate(
                [jnp.where(low, pair, zero), jnp.where(low, zero, pair)], axis=0
            )
            all_keys = jnp.concatenate(
                [window[0, pl.ds(starts[s], BLOCK), lanes] for s in slots] + pooled[:rows_parts],
                axis=0,
            )
            right = jnp.concatenate(
                [
                    jnp.concatenate(
                        [window[1, pl.ds(starts[s], BLOCK), lanes] * shown[s], shown[s]], axis=1
                    )
                    for s in slots
                ]
                + [
                    jnp.concatenate([piece, jnp.ones_like(piece)], axis=1)
                    for piece in pooled[rows_parts:]
                ],
                axis=0,
            )
            scores = lax.dot_general(
                both, all_keys, (((1,), (1,)), ((), ())), preferred_element_type=F32
            )
            row_max = jnp.max(scores, axis=-1, keepdims=True) * scale
            exponent = jnp.exp2(scores * scale - row_max).astype(BF16)
            summed = jnp.dot(exponent, right, preferred_element_type=F32)
            result = summed[:, :LANES] / summed[:, LANES:]
            attended[here, lanes] = jnp.where(low, result[:BLOCK], result[BLOCK:]).astype(BF16)

    for copy in copies[7:10]:
        copy.wait()
    residual = node_feats[...].astype(F32) + jnp.dot(
        attended[...], out_weight[...], preferred_element_type=F32
    )
    row_mean = jnp.mean(residual, axis=-1, keepdims=True)
    centered = residual - row_mean
    variance = jnp.mean(centered * centered, axis=-1, keepdims=True)
    normed = (centered * lax.rsqrt(variance + 1e-05) * norm_gain[...]).astype(BF16)
    normed_out[...] = normed
    partial_out[...] = residual + hidden_sum(normed, w_near, copies[10:])


def hidden_sum(normed, weights, copies):
    for copy in copies:
        copy.wait()
    shards = range(weights.shape[0])
    up = jnp.concatenate([weights[shard, 0] for shard in shards], axis=1)
    down = jnp.concatenate([weights[shard, 1] for shard in shards], axis=1)
    hidden = jnp.dot(normed, up, preferred_element_type=F32)
    hidden = jnp.maximum(hidden, 0.0).astype(BF16)
    return lax.dot_general(hidden, down, (((1,), (1,)), ((), ())), preferred_element_type=F32)


def finish_kernel(partial, normed, weights_in, layer_out, weights, sem):
    copies = [
        pltpu.make_async_copy(weights_in.at[shard], weights.at[shard], sem.at[shard])
        for shard in range(weights.shape[0])
    ]
    for copy in copies:
        copy.start()
    layer_out[...] = (partial[...] + hidden_sum(normed[...], weights, copies)).astype(BF16)


def along_dom(shard, by):
    length = lax.axis_size(DOM)
    pairs = [(i, i + by) for i in range(length) if 0 <= i + by < length]
    return lax.ppermute(shard, DOM, pairs)


def around(shard, axis, by):
    length = lax.axis_size(axis)
    return lax.ppermute(shard, axis, [(i, (i + by) % length) for i in range(length)])


def exchanged(parts, axes):
    return lax.all_to_all(parts, axes, 0, 0, tiled=True)


def local(
    node_feats,
    queries,
    keys,
    values,
    out_weight,
    up_weight,
    down_weight,
    norm_gain,
    tile_lists,
    virtual_of,
):
    node_rows, feat_width = queries.shape
    plane = lax.axis_size(PLANE)
    depth = lax.axis_size("z")
    near = lax.axis_size("x")
    per_part = 2 * VIRTUAL * feat_width // LANES // plane
    own_hidden = up_weight.shape[1]
    in_vmem = pl.BlockSpec(memory_space=VMEM)
    in_smem = pl.BlockSpec(memory_space=pltpu.SMEM)
    anywhere = pl.BlockSpec(memory_space=pl.ANY)
    shape = jax.ShapeDtypeStruct

    def grant(mib):
        return pltpu.CompilerParams(vmem_limit_bytes=mib * 1024 * 1024)

    def hbm(array):
        return pltpu.with_memory_space_constraint(array, pltpu.HBM)

    def vmem(array):
        return pltpu.with_memory_space_constraint(array, VMEM)

    def dma(count):
        return pltpu.SemaphoreType.DMA((count,))

    kv_shape = (2, node_rows, feat_width)
    w_shape = (2, feat_width, own_hidden)
    sums, key_value, w_0 = pl.pallas_call(
        pool_kernel,
        out_shape=(
            shape((plane, per_part, LANES), F32),
            VMEM(kv_shape, BF16),
            VMEM(w_shape, BF16),
        ),
        in_specs=[anywhere] * 5,
        out_specs=(in_vmem,) * 3,
        scratch_shapes=[VMEM((1, node_rows), jnp.int32), dma(5)],
        compiler_params=grant(6),
        name="pool",
    )(
        hbm(virtual_of.reshape(1, node_rows)),
        hbm(keys),
        hbm(values),
        hbm(up_weight),
        hbm(down_weight),
    )
    parts = exchanged(sums, PLANE)
    kv_m1 = along_dom(key_value, 1)
    kv_p1 = along_dom(key_value, -1)
    w_1 = around(w_0, "x", 1)
    w_2 = around(w_0, "x", -1)
    w_3 = around(w_0, "x", 2)

    plane_sum = pl.pallas_call(
        plane_sum_kernel,
        out_shape=shape((depth, per_part, LANES), F32),
        in_specs=[in_vmem],
        out_specs=in_vmem,
        compiler_params=grant(2),
        cost_estimate=pl.CostEstimate(
            flops=8_000_000_000, bytes_accessed=400_000, transcendentals=0
        ),
        name="plane_sum",
    )(parts)

    parts = exchanged(plane_sum, "z")
    kv_m2 = along_dom(kv_m1, 1)
    kv_p2 = along_dom(kv_p1, -1)
    token = pl.pallas_call(
        gate_kernel,
        out_shape=pltpu.HBM((8, LANES), F32),
        in_specs=[anywhere] * 3,
        out_specs=in_vmem,
        compiler_params=grant(2),
        cost_estimate=pl.CostEstimate(
            flops=4_000_000_000, bytes_accessed=6_000_000, transcendentals=2_000_000
        ),
        name="gate",
    )(plane_sum, kv_m1, kv_p1)

    pool_scale = math.sqrt(VIRTUAL / (node_rows * lax.axis_size(AXES)))
    pooled = pl.pallas_call(
        functools.partial(pooled_kernel, pool_scale),
        out_shape=shape((plane, per_part, LANES), BF16),
        in_specs=[in_vmem] + [anywhere] * 2,
        out_specs=in_vmem,
        compiler_params=grant(2),
        name="pooled",
    )(parts, hbm(token), w_3)

    virtual_kv = exchanged(pooled, PLANE)
    w_near = pl.pallas_call(
        stack_kernel,
        out_shape=pltpu.HBM((near, *w_shape), BF16),
        in_specs=[anywhere] + [in_vmem] * near,
        out_specs=in_vmem,
        compiler_params=grant(6),
        name="stack",
    )(pooled, vmem(w_0), w_1, w_2, w_3)
    w_far = around(w_near, "c", 1)

    partial, normed = pl.pallas_call(
        layer_kernel,
        out_shape=(VMEM((node_rows, feat_width), F32), VMEM((node_rows, feat_width), BF16)),
        in_specs=[in_smem, in_vmem] + [anywhere] * 11,
        out_specs=(in_vmem,) * 2,
        scratch_shapes=[
            VMEM((node_rows, feat_width), BF16),
            VMEM((2, (2 * REACH + 1) * node_rows, feat_width), BF16),
            VMEM(out_weight.shape, BF16),
            VMEM((node_rows, feat_width), BF16),
            VMEM((1, feat_width), F32),
            VMEM((near, *w_shape), BF16),
            VMEM((node_rows, feat_width), BF16),
            dma(10 + near),
        ],
        compiler_params=grant(12),
        cost_estimate=pl.CostEstimate(
            flops=400_000_000_000, bytes_accessed=6_000_000, transcendentals=2_000_000
        ),
        name="layer",
    )(
        tile_lists,
        virtual_kv,
        hbm(queries),
        hbm(keys),
        hbm(values),
        kv_m1,
        kv_p1,
        kv_p2,
        kv_m2,
        hbm(out_weight),
        hbm(node_feats),
        hbm(norm_gain.reshape(1, feat_width)),
        hbm(w_near),
    )
    return pl.pallas_call(
        finish_kernel,
        out_shape=shape((node_rows, feat_width), BF16),
        in_specs=[in_vmem, in_vmem, anywhere],
        out_specs=in_vmem,
        scratch_shapes=[VMEM((near, *w_shape), BF16), dma(near)],
        compiler_params=grant(10),
        name="finish",
    )(vmem(partial), vmem(normed), w_far)


def solution(mesh):
    group, dom = mesh.devices.shape
    fine = Mesh(mesh.devices.reshape(group // 2, 2, dom // 4, 4), AXES)
    placed = (
        P(AXES, None),
        P(AXES, None),
        P(AXES, None),
        P(AXES, None),
        P(),
        P(None, ("x", "c")),
        P(None, ("x", "c")),
        P(),
        P(AXES, None),
        P(AXES),
    )
    return jax.shard_map(
        local, mesh=fine, in_specs=placed, out_specs=P(AXES, None), check_vma=False
    )
```

```python
import functools
import math

import jax
import jax.numpy as jnp
from jax import lax
from jax.experimental import pallas as pl
from jax.experimental.pallas import tpu as pltpu
from jax.sharding import Mesh
from jax.sharding import PartitionSpec as P

HEADS = 8
BLOCK = 128
VIRTUAL = 64
REACH = 2
TMAX = 6
LANES = 128
LOG2E = 1.4426950408889634
AXES = ("x", "c", "z", "y")
DOM = ("z", "y")
PLANE = ("x", "c", "y")
VMEM = pltpu.VMEM
F32 = jnp.float32
BF16 = jnp.bfloat16


def pool_kernel(
    virtual_of_in, keys_in, values_in, up_in, down_in, sums, key_value, weights, virtual_of, sem
):
    copies = [
        pltpu.make_async_copy(source, target, sem.at[i])
        for i, (source, target) in enumerate(
            (
                (virtual_of_in, virtual_of),
                (keys_in, key_value.at[0]),
                (values_in, key_value.at[1]),
                (up_in, weights.at[0]),
                (down_in, weights.at[1]),
            )
        )
    ]
    for copy in copies:
        copy.start()
    for copy in copies[:3]:
        copy.wait()
    node_rows, feat_width = key_value.shape[1:]
    ids = lax.broadcasted_iota(jnp.int32, (VIRTUAL, node_rows), 0)
    members = jnp.where(virtual_of[...] == ids, 1.0, 0.0).astype(BF16)
    per_part = sums.shape[1]
    lane_parts = feat_width // LANES
    rows_parts = VIRTUAL // per_part
    for which in range(2):
        pooled = jnp.dot(members, key_value[which], preferred_element_type=F32)
        for row in range(rows_parts):
            for lane in range(lane_parts):
                sums[(which * rows_parts + row) * lane_parts + lane] = pooled[
                    row * per_part : (row + 1) * per_part, lane * LANES : (lane + 1) * LANES
                ]
    for copy in copies[3:]:
        copy.wait()


def plane_sum_kernel(parts, total):
    total[...] = jnp.broadcast_to(jnp.sum(parts[...], axis=0, keepdims=True), total.shape)


def pooled_kernel(scale, parts, after, after_1, pooled):
    mean = (jnp.sum(parts[...], axis=0, keepdims=True) * scale).astype(BF16)
    pooled[...] = jnp.broadcast_to(mean, pooled.shape)


def stack_kernel(after, w_0, w_1, w_2, w_3, stacked):
    for i, piece in enumerate((w_0, w_1, w_2, w_3)):
        stacked[i] = piece[...]


def gate_kernel(after, left, right, token):
    token[...] = jnp.zeros_like(token)


def layer_kernel(
    tile_lists,
    virtual_kv,
    queries_in,
    keys,
    values,
    kv_m1,
    kv_p1,
    kv_p2,
    kv_m2,
    out_weight_in,
    node_feats_in,
    norm_gain_in,
    w_near_in,
    partial_out,
    normed_out,
    queries,
    window,
    out_weight,
    node_feats,
    norm_gain,
    w_near,
    attended,
    sem,
):
    rows, feat_width = queries.shape
    near = w_near.shape[0]
    middle = REACH * rows
    moves = [
        (queries_in, queries),
        (keys, window.at[0, pl.ds(middle, rows)]),
        (values, window.at[1, pl.ds(middle, rows)]),
        (kv_m2, window.at[:, pl.ds(0, rows)]),
        (kv_p2, window.at[:, pl.ds(4 * rows, rows)]),
        (kv_m1, window.at[:, pl.ds(rows, rows)]),
        (kv_p1, window.at[:, pl.ds(3 * rows, rows)]),
        (out_weight_in, out_weight),
        (node_feats_in, node_feats),
        (norm_gain_in, norm_gain),
    ]
    moves += [(w_near_in.at[shard], w_near.at[shard]) for shard in range(near)]
    copies = [
        pltpu.make_async_copy(source, target, sem.at[i])
        for i, (source, target) in enumerate(moves)
    ]
    for copy in copies:
        copy.start()
    head_dim = feat_width // HEADS
    scale = LOG2E / math.sqrt(head_dim)
    lane_parts = feat_width // LANES
    rows_parts = VIRTUAL // virtual_kv.shape[1]
    blocks = rows // BLOCK
    low = lax.broadcasted_iota(jnp.int32, (BLOCK, LANES), 1) < head_dim
    first_block = tile_lists[0, 0] - REACH * blocks
    for copy in copies[:7]:
        copy.wait()

    def attend(block, slots, starts, shown):
        here = slice(block * BLOCK, (block + 1) * BLOCK)
        for part in range(lane_parts):
            lanes = slice(part * LANES, (part + 1) * LANES)
            pooled = [virtual_kv[r * lane_parts + part] for r in range(2 * rows_parts)]
            pair = queries[here, lanes]
            zero = jnp.zeros_like(pair)
            both = jnp.concatenate(
                [jnp.where(low, pair, zero), jnp.where(low, zero, pair)], axis=0
            )
            all_keys = jnp.concatenate(
                [window[0, pl.ds(start, BLOCK), lanes] for start in starts[:slots]]
                + pooled[:rows_parts],
                axis=0,
            )
            right = jnp.concatenate(
                [
                    jnp.concatenate(
                        [window[1, pl.ds(start, BLOCK), lanes] * there, there], axis=1
                    )
                    for start, there in zip(starts[:slots], shown)
                ]
                + [
                    jnp.concatenate([piece, jnp.ones_like(piece)], axis=1)
                    for piece in pooled[rows_parts:]
                ],
                axis=0,
            )
            scores = lax.dot_general(
                both, all_keys, (((1,), (1,)), ((), ())), preferred_element_type=F32
            )
            row_max = jnp.max(scores, axis=-1, keepdims=True) * scale
            exponent = jnp.exp2(scores * scale - row_max).astype(BF16)
            summed = jnp.dot(exponent, right, preferred_element_type=F32)
            result = summed[:, :LANES] / summed[:, LANES:]
            attended[here, lanes] = jnp.where(low, result[:BLOCK], result[BLOCK:]).astype(BF16)

    for block in range(blocks):
        own = tile_lists[block, 0]
        starts = []
        shown = []
        for slot in range(TMAX):
            tile = tile_lists[block, slot]
            there = tile >= 0
            place = jnp.where(there, tile, own) - first_block
            starts.append(pl.multiple_of(place * BLOCK, BLOCK))
            shown.append(jnp.full((BLOCK, LANES), jnp.where(there, 1.0, 0.0), F32).astype(BF16))
        for slots in range(2, TMAX + 1, 2):
            needed = tile_lists[block, slots - 2] >= 0
            if slots < TMAX:
                needed = jnp.logical_and(needed, tile_lists[block, slots] < 0)
            pl.when(needed)(functools.partial(attend, block, slots, starts, shown))

    for copy in copies[7:10]:
        copy.wait()
    residual = node_feats[...].astype(F32) + jnp.dot(
        attended[...], out_weight[...], preferred_element_type=F32
    )
    row_mean = jnp.mean(residual, axis=-1, keepdims=True)
    centered = residual - row_mean
    variance = jnp.mean(centered * centered, axis=-1, keepdims=True)
    normed = (centered * lax.rsqrt(variance + 1e-05) * norm_gain[...]).astype(BF16)
    normed_out[...] = normed
    partial_out[...] = residual + hidden_sum(normed, w_near, copies[10:])


def hidden_sum(normed, weights, copies):
    for copy in copies:
        copy.wait()
    shards = range(weights.shape[0])
    up = jnp.concatenate([weights[shard, 0] for shard in shards], axis=1)
    down = jnp.concatenate([weights[shard, 1] for shard in shards], axis=1)
    hidden = jnp.dot(normed, up, preferred_element_type=F32)
    hidden = jnp.maximum(hidden, 0.0).astype(BF16)
    return lax.dot_general(hidden, down, (((1,), (1,)), ((), ())), preferred_element_type=F32)


def finish_kernel(partial, normed, weights, layer_out):
    layer_out[...] = (partial[...] + hidden_sum(normed[...], weights, ())).astype(BF16)


def along_dom(shard, by):
    length = lax.axis_size(DOM)
    pairs = [(i, i + by) for i in range(length) if 0 <= i + by < length]
    return lax.ppermute(shard, DOM, pairs)


def around(shard, axis, by):
    length = lax.axis_size(axis)
    return lax.ppermute(shard, axis, [(i, (i + by) % length) for i in range(length)])


def exchanged(parts, axes):
    return lax.all_to_all(parts, axes, 0, 0, tiled=True)


def local(
    node_feats,
    queries,
    keys,
    values,
    out_weight,
    up_weight,
    down_weight,
    norm_gain,
    tile_lists,
    virtual_of,
):
    node_rows, feat_width = queries.shape
    plane = lax.axis_size(PLANE)
    depth = lax.axis_size("z")
    near = lax.axis_size("x")
    per_part = 2 * VIRTUAL * feat_width // LANES // plane
    own_hidden = up_weight.shape[1]
    in_vmem = pl.BlockSpec(memory_space=VMEM)
    in_smem = pl.BlockSpec(memory_space=pltpu.SMEM)
    anywhere = pl.BlockSpec(memory_space=pl.ANY)
    shape = jax.ShapeDtypeStruct

    def grant(mib):
        return pltpu.CompilerParams(vmem_limit_bytes=mib * 1024 * 1024)

    def hbm(array):
        return pltpu.with_memory_space_constraint(array, pltpu.HBM)

    def vmem(array):
        return pltpu.with_memory_space_constraint(array, VMEM)

    def dma(count):
        return pltpu.SemaphoreType.DMA((count,))

    kv_shape = (2, node_rows, feat_width)
    w_shape = (2, feat_width, own_hidden)
    sums, key_value, w_0 = pl.pallas_call(
        pool_kernel,
        out_shape=(
            VMEM((plane, per_part, LANES), F32),
            VMEM(kv_shape, BF16),
            VMEM(w_shape, BF16),
        ),
        in_specs=[anywhere] * 5,
        out_specs=(in_vmem,) * 3,
        scratch_shapes=[VMEM((1, node_rows), jnp.int32), dma(5)],
        compiler_params=grant(6),
        name="pool",
    )(
        hbm(virtual_of.reshape(1, node_rows)),
        hbm(keys),
        hbm(values),
        hbm(up_weight),
        hbm(down_weight),
    )
    parts = exchanged(sums, PLANE)
    kv_m1 = along_dom(key_value, 1)
    kv_p1 = along_dom(key_value, -1)
    w_1 = around(w_0, "x", 1)
    w_2 = around(w_0, "x", -1)
    w_3 = around(w_0, "x", 2)

    plane_sum = pl.pallas_call(
        plane_sum_kernel,
        out_shape=VMEM((depth, per_part, LANES), F32),
        in_specs=[in_vmem],
        out_specs=in_vmem,
        compiler_params=grant(2),
        cost_estimate=pl.CostEstimate(
            flops=8_000_000_000, bytes_accessed=400_000, transcendentals=0
        ),
        name="plane_sum",
    )(parts)

    parts = exchanged(plane_sum, "z")
    kv_m2 = along_dom(kv_m1, 1)
    kv_p2 = along_dom(kv_p1, -1)
    token = pl.pallas_call(
        gate_kernel,
        out_shape=VMEM((8, LANES), F32),
        in_specs=[anywhere] * 3,
        out_specs=in_vmem,
        compiler_params=grant(2),
        cost_estimate=pl.CostEstimate(
            flops=4_000_000_000, bytes_accessed=6_000_000, transcendentals=2_000_000
        ),
        name="gate",
    )(plane_sum, kv_m1, kv_p1)

    pool_scale = math.sqrt(VIRTUAL / (node_rows * lax.axis_size(AXES)))
    pooled = pl.pallas_call(
        functools.partial(pooled_kernel, pool_scale),
        out_shape=VMEM((plane, per_part, LANES), BF16),
        in_specs=[in_vmem] + [anywhere] * 2,
        out_specs=in_vmem,
        compiler_params=grant(2),
        name="pooled",
    )(parts, vmem(token), w_3)

    virtual_kv = exchanged(pooled, PLANE)
    w_near = pl.pallas_call(
        stack_kernel,
        out_shape=pltpu.HBM((near, *w_shape), BF16),
        in_specs=[anywhere] + [in_vmem] * near,
        out_specs=in_vmem,
        compiler_params=grant(6),
        name="stack",
    )(pooled, vmem(w_0), w_1, w_2, w_3)
    w_far = around(w_near, "c", 1)

    partial, normed = pl.pallas_call(
        layer_kernel,
        out_shape=(VMEM((node_rows, feat_width), F32), VMEM((node_rows, feat_width), BF16)),
        in_specs=[in_smem, in_vmem] + [anywhere] * 11,
        out_specs=(in_vmem,) * 2,
        scratch_shapes=[
            VMEM((node_rows, feat_width), BF16),
            VMEM((2, (2 * REACH + 1) * node_rows, feat_width), BF16),
            VMEM(out_weight.shape, BF16),
            VMEM((node_rows, feat_width), BF16),
            VMEM((1, feat_width), F32),
            VMEM((near, *w_shape), BF16),
            VMEM((node_rows, feat_width), BF16),
            dma(10 + near),
        ],
        compiler_params=grant(12),
        cost_estimate=pl.CostEstimate(
            flops=400_000_000_000, bytes_accessed=6_000_000, transcendentals=2_000_000
        ),
        name="layer",
    )(
        tile_lists,
        virtual_kv,
        hbm(queries),
        hbm(keys),
        hbm(values),
        kv_m1,
        kv_p1,
        kv_p2,
        kv_m2,
        hbm(out_weight),
        hbm(node_feats),
        hbm(norm_gain.reshape(1, feat_width)),
        hbm(w_near),
    )
    return pl.pallas_call(
        finish_kernel,
        out_shape=shape((node_rows, feat_width), BF16),
        in_specs=[in_vmem] * 3,
        out_specs=in_vmem,
        compiler_params=grant(8),
        name="finish",
    )(vmem(partial), vmem(normed), vmem(w_far))


def solution(mesh):
    group, dom = mesh.devices.shape
    fine = Mesh(mesh.devices.reshape(group // 2, 2, dom // 4, 4), AXES)
    placed = (
        P(AXES, None),
        P(AXES, None),
        P(AXES, None),
        P(AXES, None),
        P(),
        P(None, ("x", "c")),
        P(None, ("x", "c")),
        P(),
        P(AXES, None),
        P(AXES),
    )
    return jax.shard_map(
        local, mesh=fine, in_specs=placed, out_specs=P(AXES, None), check_vma=False
    )
```

```python
import functools
import math

import jax
import jax.numpy as jnp
from jax import lax
from jax.experimental import pallas as pl
from jax.experimental.pallas import tpu as pltpu
from jax.sharding import Mesh
from jax.sharding import PartitionSpec as P

HEADS = 8
BLOCK = 128
VIRTUAL = 64
REACH = 2
TMAX = 6
LANES = 128
LOG2E = 1.4426950408889634
AXES = ("x", "c", "z", "y")
DOM = ("z", "y")
PLANE = ("x", "c", "y")
VMEM = pltpu.VMEM
F32 = jnp.float32
BF16 = jnp.bfloat16


def pool_kernel(
    virtual_of_in, keys_in, values_in, up_in, down_in, sums, key_value, weights, virtual_of, sem
):
    copies = [
        pltpu.make_async_copy(source, target, sem.at[i])
        for i, (source, target) in enumerate(
            (
                (virtual_of_in, virtual_of),
                (keys_in, key_value.at[0]),
                (values_in, key_value.at[1]),
                (up_in, weights.at[0]),
                (down_in, weights.at[1]),
            )
        )
    ]
    for copy in copies:
        copy.start()
    for copy in copies[:3]:
        copy.wait()
    node_rows, feat_width = key_value.shape[1:]
    ids = lax.broadcasted_iota(jnp.int32, (VIRTUAL, node_rows), 0)
    members = jnp.where(virtual_of[...] == ids, 1.0, 0.0).astype(BF16)
    per_part = sums.shape[1]
    lane_parts = feat_width // LANES
    rows_parts = VIRTUAL // per_part
    for which in range(2):
        pooled = jnp.dot(members, key_value[which], preferred_element_type=F32)
        for row in range(rows_parts):
            for lane in range(lane_parts):
                sums[(which * rows_parts + row) * lane_parts + lane] = pooled[
                    row * per_part : (row + 1) * per_part, lane * LANES : (lane + 1) * LANES
                ]
    for copy in copies[3:]:
        copy.wait()


def plane_sum_kernel(parts, total):
    total[...] = jnp.broadcast_to(jnp.sum(parts[...], axis=0, keepdims=True), total.shape)


def pooled_kernel(scale, parts, after, after_1, pooled):
    mean = (jnp.sum(parts[...], axis=0, keepdims=True) * scale).astype(BF16)
    pooled[...] = jnp.broadcast_to(mean, pooled.shape)


def stack_kernel(after, w_0, w_1, w_2, w_3, stacked):
    for i, piece in enumerate((w_0, w_1, w_2, w_3)):
        stacked[i] = piece[...]


def gate_kernel(after, left, right, token):
    token[...] = jnp.zeros_like(token)


def layer_kernel(
    tile_lists,
    virtual_kv,
    queries_in,
    keys,
    values,
    kv_m1,
    kv_p1,
    kv_p2,
    kv_m2,
    out_weight_in,
    node_feats_in,
    norm_gain_in,
    w_near_in,
    partial_out,
    normed_out,
    queries,
    window,
    out_weight,
    node_feats,
    norm_gain,
    w_near,
    attended,
    sem,
):
    rows, feat_width = queries.shape
    near = w_near.shape[0]
    middle = REACH * rows
    moves = [
        (queries_in, queries),
        (keys, window.at[0, pl.ds(middle, rows)]),
        (values, window.at[1, pl.ds(middle, rows)]),
        (kv_m2, window.at[:, pl.ds(0, rows)]),
        (kv_p2, window.at[:, pl.ds(4 * rows, rows)]),
        (kv_m1, window.at[:, pl.ds(rows, rows)]),
        (kv_p1, window.at[:, pl.ds(3 * rows, rows)]),
        (out_weight_in, out_weight),
        (node_feats_in, node_feats),
        (norm_gain_in, norm_gain),
    ]
    moves += [(w_near_in.at[shard], w_near.at[shard]) for shard in range(near)]
    copies = [
        pltpu.make_async_copy(source, target, sem.at[i])
        for i, (source, target) in enumerate(moves)
    ]
    for copy in copies:
        copy.start()
    head_dim = feat_width // HEADS
    scale = LOG2E / math.sqrt(head_dim)
    lane_parts = feat_width // LANES
    rows_parts = VIRTUAL // virtual_kv.shape[1]
    blocks = rows // BLOCK
    low = lax.broadcasted_iota(jnp.int32, (BLOCK, LANES), 1) < head_dim
    first_block = tile_lists[0, 0] - REACH * blocks
    for copy in copies[:7]:
        copy.wait()

    def attend(block, slots, starts, shown):
        here = slice(block * BLOCK, (block + 1) * BLOCK)
        for part in range(lane_parts):
            lanes = slice(part * LANES, (part + 1) * LANES)
            pooled = [virtual_kv[r * lane_parts + part] for r in range(2 * rows_parts)]
            pair = queries[here, lanes]
            zero = jnp.zeros_like(pair)
            both = jnp.concatenate(
                [jnp.where(low, pair, zero), jnp.where(low, zero, pair)], axis=0
            )
            all_keys = jnp.concatenate(
                [window[0, pl.ds(start, BLOCK), lanes] for start in starts[:slots]]
                + pooled[:rows_parts],
                axis=0,
            )
            right = jnp.concatenate(
                [
                    jnp.concatenate(
                        [window[1, pl.ds(start, BLOCK), lanes] * there, there], axis=1
                    )
                    for start, there in zip(starts[:slots], shown)
                ]
                + [
                    jnp.concatenate([piece, jnp.ones_like(piece)], axis=1)
                    for piece in pooled[rows_parts:]
                ],
                axis=0,
            )
            scores = lax.dot_general(
                both, all_keys, (((1,), (1,)), ((), ())), preferred_element_type=F32
            )
            row_max = jnp.max(scores, axis=-1, keepdims=True) * scale
            exponent = jnp.exp2(scores * scale - row_max).astype(BF16)
            summed = jnp.dot(exponent, right, preferred_element_type=F32)
            result = summed[:, :LANES] / summed[:, LANES:]
            attended[here, lanes] = jnp.where(low, result[:BLOCK], result[BLOCK:]).astype(BF16)

    for block in range(blocks):
        own = tile_lists[block, 0]
        starts = []
        shown = []
        for slot in range(TMAX):
            tile = tile_lists[block, slot]
            there = tile >= 0
            place = jnp.where(there, tile, own) - first_block
            starts.append(pl.multiple_of(place * BLOCK, BLOCK))
            shown.append(jnp.full((BLOCK, LANES), jnp.where(there, 1.0, 0.0), F32).astype(BF16))
        for slots in range(2, TMAX + 1, 2):
            needed = tile_lists[block, slots - 2] >= 0
            if slots < TMAX:
                needed = jnp.logical_and(needed, tile_lists[block, slots] < 0)
            pl.when(needed)(functools.partial(attend, block, slots, starts, shown))

    for copy in copies[7:10]:
        copy.wait()
    residual = node_feats[...].astype(F32) + jnp.dot(
        attended[...], out_weight[...], preferred_element_type=F32
    )
    row_mean = jnp.mean(residual, axis=-1, keepdims=True)
    centered = residual - row_mean
    variance = jnp.mean(centered * centered, axis=-1, keepdims=True)
    normed = (centered * lax.rsqrt(variance + 1e-05) * norm_gain[...]).astype(BF16)
    normed_out[...] = normed
    partial_out[...] = residual + hidden_sum(normed, w_near, copies[10:])


def hidden_sum(normed, weights, copies):
    for copy in copies:
        copy.wait()
    shards = range(weights.shape[0])
    up = jnp.concatenate([weights[shard, 0] for shard in shards], axis=1)
    down = jnp.concatenate([weights[shard, 1] for shard in shards], axis=1)
    hidden = jnp.dot(normed, up, preferred_element_type=F32)
    hidden = jnp.maximum(hidden, 0.0).astype(BF16)
    return lax.dot_general(hidden, down, (((1,), (1,)), ((), ())), preferred_element_type=F32)


def finish_kernel(partial, normed, weights, layer_out):
    layer_out[...] = (partial[...] + hidden_sum(normed[...], weights, ())).astype(BF16)


def along_dom(shard, by):
    length = lax.axis_size(DOM)
    pairs = [(i, i + by) for i in range(length) if 0 <= i + by < length]
    return lax.ppermute(shard, DOM, pairs)


def around(shard, axis, by):
    length = lax.axis_size(axis)
    return lax.ppermute(shard, axis, [(i, (i + by) % length) for i in range(length)])


def exchanged(parts, axes):
    return lax.all_to_all(parts, axes, 0, 0, tiled=True)


def local(
    node_feats,
    queries,
    keys,
    values,
    out_weight,
    up_weight,
    down_weight,
    norm_gain,
    tile_lists,
    virtual_of,
):
    node_rows, feat_width = queries.shape
    plane = lax.axis_size(PLANE)
    depth = lax.axis_size("z")
    near = lax.axis_size("x")
    per_part = 2 * VIRTUAL * feat_width // LANES // plane
    own_hidden = up_weight.shape[1]
    in_vmem = pl.BlockSpec(memory_space=VMEM)
    in_smem = pl.BlockSpec(memory_space=pltpu.SMEM)
    anywhere = pl.BlockSpec(memory_space=pl.ANY)
    shape = jax.ShapeDtypeStruct

    def grant(mib):
        return pltpu.CompilerParams(vmem_limit_bytes=mib * 1024 * 1024)

    def hbm(array):
        return pltpu.with_memory_space_constraint(array, pltpu.HBM)

    def vmem(array):
        return pltpu.with_memory_space_constraint(array, VMEM)

    def dma(count):
        return pltpu.SemaphoreType.DMA((count,))

    kv_shape = (2, node_rows, feat_width)
    w_shape = (2, feat_width, own_hidden)
    sums, key_value, w_0 = pl.pallas_call(
        pool_kernel,
        out_shape=(
            VMEM((plane, per_part, LANES), F32),
            VMEM(kv_shape, BF16),
            VMEM(w_shape, BF16),
        ),
        in_specs=[anywhere] * 5,
        out_specs=(in_vmem,) * 3,
        scratch_shapes=[VMEM((1, node_rows), jnp.int32), dma(5)],
        compiler_params=grant(6),
        name="pool",
    )(
        hbm(virtual_of.reshape(1, node_rows)),
        hbm(keys),
        hbm(values),
        hbm(up_weight),
        hbm(down_weight),
    )
    parts = exchanged(sums, PLANE)
    kv_m1 = along_dom(key_value, 1)
    kv_p1 = along_dom(key_value, -1)
    w_1 = around(w_0, "x", 1)
    w_2 = around(w_0, "x", -1)
    w_3 = around(w_1, "x", 1)

    plane_sum = pl.pallas_call(
        plane_sum_kernel,
        out_shape=VMEM((depth, per_part, LANES), F32),
        in_specs=[in_vmem],
        out_specs=in_vmem,
        compiler_params=grant(2),
        cost_estimate=pl.CostEstimate(
            flops=8_000_000_000, bytes_accessed=400_000, transcendentals=0
        ),
        name="plane_sum",
    )(parts)

    parts = exchanged(plane_sum, "z")
    kv_m2 = along_dom(kv_m1, 1)
    kv_p2 = along_dom(kv_p1, -1)
    token = pl.pallas_call(
        gate_kernel,
        out_shape=VMEM((8, LANES), F32),
        in_specs=[anywhere] * 3,
        out_specs=in_vmem,
        compiler_params=grant(2),
        cost_estimate=pl.CostEstimate(
            flops=4_000_000_000, bytes_accessed=6_000_000, transcendentals=2_000_000
        ),
        name="gate",
    )(plane_sum, kv_m1, kv_p1)

    pool_scale = math.sqrt(VIRTUAL / (node_rows * lax.axis_size(AXES)))
    pooled = pl.pallas_call(
        functools.partial(pooled_kernel, pool_scale),
        out_shape=VMEM((plane, per_part, LANES), BF16),
        in_specs=[in_vmem] + [anywhere] * 2,
        out_specs=in_vmem,
        compiler_params=grant(2),
        name="pooled",
    )(parts, vmem(token), w_1)

    virtual_kv = exchanged(pooled, PLANE)
    w_near = pl.pallas_call(
        stack_kernel,
        out_shape=pltpu.HBM((near, *w_shape), BF16),
        in_specs=[anywhere] + [in_vmem] * near,
        out_specs=in_vmem,
        compiler_params=grant(6),
        name="stack",
    )(pooled, vmem(w_0), w_1, w_2, w_3)
    w_far = around(w_near, "c", 1)

    partial, normed = pl.pallas_call(
        layer_kernel,
        out_shape=(VMEM((node_rows, feat_width), F32), VMEM((node_rows, feat_width), BF16)),
        in_specs=[in_smem, in_vmem] + [anywhere] * 11,
        out_specs=(in_vmem,) * 2,
        scratch_shapes=[
            VMEM((node_rows, feat_width), BF16),
            VMEM((2, (2 * REACH + 1) * node_rows, feat_width), BF16),
            VMEM(out_weight.shape, BF16),
            VMEM((node_rows, feat_width), BF16),
            VMEM((1, feat_width), F32),
            VMEM((near, *w_shape), BF16),
            VMEM((node_rows, feat_width), BF16),
            dma(10 + near),
        ],
        compiler_params=grant(12),
        cost_estimate=pl.CostEstimate(
            flops=400_000_000_000, bytes_accessed=6_000_000, transcendentals=2_000_000
        ),
        name="layer",
    )(
        tile_lists,
        virtual_kv,
        hbm(queries),
        hbm(keys),
        hbm(values),
        kv_m1,
        kv_p1,
        kv_p2,
        kv_m2,
        hbm(out_weight),
        hbm(node_feats),
        hbm(norm_gain.reshape(1, feat_width)),
        hbm(w_near),
    )
    return pl.pallas_call(
        finish_kernel,
        out_shape=shape((node_rows, feat_width), BF16),
        in_specs=[in_vmem] * 3,
        out_specs=in_vmem,
        compiler_params=grant(8),
        name="finish",
    )(vmem(partial), vmem(normed), vmem(w_far))


def solution(mesh):
    group, dom = mesh.devices.shape
    fine = Mesh(mesh.devices.reshape(group // 2, 2, dom // 4, 4), AXES)
    placed = (
        P(AXES, None),
        P(AXES, None),
        P(AXES, None),
        P(AXES, None),
        P(),
        P(None, ("x", "c")),
        P(None, ("x", "c")),
        P(),
        P(AXES, None),
        P(AXES),
    )
    return jax.shard_map(
        local, mesh=fine, in_specs=placed, out_specs=P(AXES, None), check_vma=False
    )
```

```python
import functools
import math

import jax
import jax.numpy as jnp
from jax import lax
from jax.experimental import pallas as pl
from jax.experimental.pallas import tpu as pltpu
from jax.sharding import Mesh
from jax.sharding import PartitionSpec as P

HEADS = 8
BLOCK = 128
VIRTUAL = 64
REACH = 2
TMAX = 6
LANES = 128
LOG2E = 1.4426950408889634
AXES = ("x", "c", "z", "y")
DOM = ("z", "y")
PLANE = ("x", "c", "y")
VMEM = pltpu.VMEM
F32 = jnp.float32
BF16 = jnp.bfloat16


def pool_kernel(
    virtual_of_in, keys_in, values_in, up_in, down_in, sums, key_value, weights, virtual_of, sem
):
    copies = [
        pltpu.make_async_copy(source, target, sem.at[i])
        for i, (source, target) in enumerate(
            (
                (virtual_of_in, virtual_of),
                (keys_in, key_value.at[0]),
                (values_in, key_value.at[1]),
                (up_in, weights.at[0]),
                (down_in, weights.at[1]),
            )
        )
    ]
    for copy in copies:
        copy.start()
    for copy in copies[:3]:
        copy.wait()
    node_rows, feat_width = key_value.shape[1:]
    ids = lax.broadcasted_iota(jnp.int32, (VIRTUAL, node_rows), 0)
    members = jnp.where(virtual_of[...] == ids, 1.0, 0.0).astype(BF16)
    per_part = sums.shape[1]
    lane_parts = feat_width // LANES
    rows_parts = VIRTUAL // per_part
    for which in range(2):
        pooled = jnp.dot(members, key_value[which], preferred_element_type=F32)
        for row in range(rows_parts):
            for lane in range(lane_parts):
                sums[(which * rows_parts + row) * lane_parts + lane] = pooled[
                    row * per_part : (row + 1) * per_part, lane * LANES : (lane + 1) * LANES
                ]
    for copy in copies[3:]:
        copy.wait()


def plane_sum_kernel(parts, total):
    total[...] = jnp.broadcast_to(jnp.sum(parts[...], axis=0, keepdims=True), total.shape)


def pooled_kernel(scale, parts, after, after_1, pooled):
    mean = (jnp.sum(parts[...], axis=0, keepdims=True) * scale).astype(BF16)
    pooled[...] = jnp.broadcast_to(mean, pooled.shape)


def stack_kernel(after, w_0, w_1, w_2, w_3, stacked):
    for i, piece in enumerate((w_0, w_1, w_2, w_3)):
        stacked[i] = piece[...]


def gate_kernel(after, left, right, token):
    token[...] = jnp.zeros_like(token)


def layer_kernel(
    tile_lists,
    virtual_kv,
    queries_in,
    keys,
    values,
    kv_m1,
    kv_p1,
    kv_p2,
    kv_m2,
    out_weight_in,
    node_feats_in,
    norm_gain_in,
    w_near_in,
    partial_out,
    normed_out,
    queries,
    window,
    out_weight,
    node_feats,
    norm_gain,
    w_near,
    attended,
    sem,
):
    rows, feat_width = queries.shape
    middle = REACH * rows
    moves = [
        (queries_in, queries),
        (keys, window.at[0, pl.ds(middle, rows)]),
        (values, window.at[1, pl.ds(middle, rows)]),
        (kv_m2, window.at[:, pl.ds(0, rows)]),
        (kv_p2, window.at[:, pl.ds(4 * rows, rows)]),
        (kv_m1, window.at[:, pl.ds(rows, rows)]),
        (kv_p1, window.at[:, pl.ds(3 * rows, rows)]),
        (out_weight_in, out_weight),
        (node_feats_in, node_feats),
        (norm_gain_in, norm_gain),
    ]
    moves.append((w_near_in, w_near))
    copies = [
        pltpu.make_async_copy(source, target, sem.at[i])
        for i, (source, target) in enumerate(moves)
    ]
    for copy in copies:
        copy.start()
    head_dim = feat_width // HEADS
    scale = LOG2E / math.sqrt(head_dim)
    lane_parts = feat_width // LANES
    rows_parts = VIRTUAL // virtual_kv.shape[1]
    blocks = rows // BLOCK
    low = lax.broadcasted_iota(jnp.int32, (BLOCK, LANES), 1) < head_dim
    first_block = tile_lists[0, 0] - REACH * blocks
    for copy in copies[:7]:
        copy.wait()

    ones = jnp.ones((BLOCK, LANES), BF16)

    def attend(block, slots, starts, shown):
        last = jnp.full((BLOCK, LANES), jnp.where(shown[slots - 1], 1.0, 0.0), F32).astype(BF16)
        here = slice(block * BLOCK, (block + 1) * BLOCK)
        for part in range(lane_parts):
            lanes = slice(part * LANES, (part + 1) * LANES)
            pooled = [virtual_kv[r * lane_parts + part] for r in range(2 * rows_parts)]
            pair = queries[here, lanes]
            zero = jnp.zeros_like(pair)
            both = jnp.concatenate(
                [jnp.where(low, pair, zero), jnp.where(low, zero, pair)], axis=0
            )
            all_keys = jnp.concatenate(
                [window[0, pl.ds(start, BLOCK), lanes] for start in starts[:slots]]
                + pooled[:rows_parts],
                axis=0,
            )
            sides = [(window[1, pl.ds(start, BLOCK), lanes], ones) for start in starts[:slots]]
            sides[-1] = (sides[-1][0] * last, last)
            sides += [(piece, jnp.ones_like(piece)) for piece in pooled[rows_parts:]]
            right = jnp.concatenate([jnp.concatenate(side, axis=1) for side in sides], axis=0)
            scores = lax.dot_general(
                both, all_keys, (((1,), (1,)), ((), ())), preferred_element_type=F32
            )
            row_max = jnp.max(scores, axis=-1, keepdims=True) * scale
            exponent = jnp.exp2(scores * scale - row_max).astype(BF16)
            summed = jnp.dot(exponent, right, preferred_element_type=F32)
            result = summed[:, :LANES] / summed[:, LANES:]
            attended[here, lanes] = jnp.where(low, result[:BLOCK], result[BLOCK:]).astype(BF16)

    for block in range(blocks):
        own = tile_lists[block, 0]
        starts = []
        shown = []
        for slot in range(TMAX):
            tile = tile_lists[block, slot]
            there = tile >= 0
            place = jnp.where(there, tile, own) - first_block
            starts.append(pl.multiple_of(place * BLOCK, BLOCK))
            shown.append(there)
        for slots in range(2, TMAX + 1, 2):
            needed = tile_lists[block, slots - 2] >= 0
            if slots < TMAX:
                needed = jnp.logical_and(needed, tile_lists[block, slots] < 0)
            pl.when(needed)(functools.partial(attend, block, slots, starts, shown))

    for copy in copies[7:10]:
        copy.wait()
    residual = node_feats[...].astype(F32) + jnp.dot(
        attended[...], out_weight[...], preferred_element_type=F32
    )
    row_mean = jnp.mean(residual, axis=-1, keepdims=True)
    centered = residual - row_mean
    variance = jnp.mean(centered * centered, axis=-1, keepdims=True)
    normed = (centered * lax.rsqrt(variance + 1e-05) * norm_gain[...]).astype(BF16)
    normed_out[...] = normed
    copies[10].wait()
    hidden = hidden_units(normed, w_near.at[:, 0])
    partial_out[...] = residual + projected(hidden, w_near.at[:, 1])


def side_by_side(shards):
    return jnp.concatenate([shards[shard] for shard in range(shards.shape[0])], axis=1)


def hidden_units(normed, up):
    hidden = jnp.dot(normed, side_by_side(up), preferred_element_type=F32)
    return jnp.maximum(hidden, 0.0).astype(BF16)


def projected(hidden, down):
    return lax.dot_general(
        hidden, side_by_side(down), (((1,), (1,)), ((), ())), preferred_element_type=F32
    )


def finish_kernel(partial, normed, weights_in, layer_out, up, down, sem):
    copies = [
        pltpu.make_async_copy(weights_in.at[:, which], target, sem.at[which])
        for which, target in enumerate((up, down))
    ]
    for copy in copies:
        copy.start()
    copies[0].wait()
    hidden = hidden_units(normed[...], up)
    copies[1].wait()
    layer_out[...] = (partial[...] + projected(hidden, down)).astype(BF16)


def along_dom(shard, by):
    length = lax.axis_size(DOM)
    pairs = [(i, i + by) for i in range(length) if 0 <= i + by < length]
    return lax.ppermute(shard, DOM, pairs)


def around(shard, axis, by):
    length = lax.axis_size(axis)
    return lax.ppermute(shard, axis, [(i, (i + by) % length) for i in range(length)])


def exchanged(parts, axes):
    return lax.all_to_all(parts, axes, 0, 0, tiled=True)


def local(
    node_feats,
    queries,
    keys,
    values,
    out_weight,
    up_weight,
    down_weight,
    norm_gain,
    tile_lists,
    virtual_of,
):
    node_rows, feat_width = queries.shape
    plane = lax.axis_size(PLANE)
    depth = lax.axis_size("z")
    near = lax.axis_size("x")
    per_part = 2 * VIRTUAL * feat_width // LANES // plane
    own_hidden = up_weight.shape[1]
    in_vmem = pl.BlockSpec(memory_space=VMEM)
    in_smem = pl.BlockSpec(memory_space=pltpu.SMEM)
    anywhere = pl.BlockSpec(memory_space=pl.ANY)
    shape = jax.ShapeDtypeStruct

    def grant(mib):
        return pltpu.CompilerParams(vmem_limit_bytes=mib * 1024 * 1024)

    def hbm(array):
        return pltpu.with_memory_space_constraint(array, pltpu.HBM)

    def vmem(array):
        return pltpu.with_memory_space_constraint(array, VMEM)

    def dma(count):
        return pltpu.SemaphoreType.DMA((count,))

    kv_shape = (2, node_rows, feat_width)
    w_shape = (2, feat_width, own_hidden)
    sums, key_value, w_0 = pl.pallas_call(
        pool_kernel,
        out_shape=(
            VMEM((plane, per_part, LANES), F32),
            VMEM(kv_shape, BF16),
            VMEM(w_shape, BF16),
        ),
        in_specs=[anywhere] * 5,
        out_specs=(in_vmem,) * 3,
        scratch_shapes=[VMEM((1, node_rows), jnp.int32), dma(5)],
        compiler_params=grant(6),
        name="pool",
    )(
        hbm(virtual_of.reshape(1, node_rows)),
        hbm(keys),
        hbm(values),
        hbm(up_weight),
        hbm(down_weight),
    )
    parts = exchanged(sums, PLANE)
    kv_m1 = along_dom(key_value, 1)
    kv_p1 = along_dom(key_value, -1)
    w_1 = around(w_0, "x", 1)
    w_2 = around(w_0, "x", -1)
    w_3 = around(w_1, "x", 1)

    plane_sum = pl.pallas_call(
        plane_sum_kernel,
        out_shape=VMEM((depth, per_part, LANES), F32),
        in_specs=[in_vmem],
        out_specs=in_vmem,
        compiler_params=grant(2),
        cost_estimate=pl.CostEstimate(
            flops=8_000_000_000, bytes_accessed=400_000, transcendentals=0
        ),
        name="plane_sum",
    )(parts)

    parts = exchanged(plane_sum, "z")
    kv_m2 = along_dom(kv_m1, 1)
    kv_p2 = along_dom(kv_p1, -1)
    token = pl.pallas_call(
        gate_kernel,
        out_shape=VMEM((8, LANES), F32),
        in_specs=[anywhere] * 3,
        out_specs=in_vmem,
        compiler_params=grant(2),
        cost_estimate=pl.CostEstimate(
            flops=4_000_000_000, bytes_accessed=6_000_000, transcendentals=2_000_000
        ),
        name="gate",
    )(plane_sum, kv_m1, kv_p1)

    pool_scale = math.sqrt(VIRTUAL / (node_rows * lax.axis_size(AXES)))
    pooled = pl.pallas_call(
        functools.partial(pooled_kernel, pool_scale),
        out_shape=VMEM((plane, per_part, LANES), BF16),
        in_specs=[in_vmem] + [anywhere] * 2,
        out_specs=in_vmem,
        compiler_params=grant(2),
        name="pooled",
    )(parts, vmem(token), w_1)

    virtual_kv = exchanged(pooled, PLANE)
    w_near = pl.pallas_call(
        stack_kernel,
        out_shape=pltpu.HBM((near, *w_shape), BF16),
        in_specs=[anywhere] + [in_vmem] * near,
        out_specs=in_vmem,
        compiler_params=grant(6),
        name="stack",
    )(pooled, vmem(w_0), w_1, w_2, w_3)
    w_far = around(w_near, "c", 1)

    partial, normed = pl.pallas_call(
        layer_kernel,
        out_shape=(VMEM((node_rows, feat_width), F32), VMEM((node_rows, feat_width), BF16)),
        in_specs=[in_smem, in_vmem] + [anywhere] * 11,
        out_specs=(in_vmem,) * 2,
        scratch_shapes=[
            VMEM((node_rows, feat_width), BF16),
            VMEM((2, (2 * REACH + 1) * node_rows, feat_width), BF16),
            VMEM(out_weight.shape, BF16),
            VMEM((node_rows, feat_width), BF16),
            VMEM((1, feat_width), F32),
            VMEM((near, *w_shape), BF16),
            VMEM((node_rows, feat_width), BF16),
            dma(11),
        ],
        compiler_params=grant(10),
        cost_estimate=pl.CostEstimate(
            flops=400_000_000_000, bytes_accessed=6_000_000, transcendentals=2_000_000
        ),
        name="layer",
    )(
        tile_lists,
        virtual_kv,
        hbm(queries),
        hbm(keys),
        hbm(values),
        kv_m1,
        kv_p1,
        kv_p2,
        kv_m2,
        hbm(out_weight),
        hbm(node_feats),
        hbm(norm_gain.reshape(1, feat_width)),
        hbm(w_near),
    )
    return pl.pallas_call(
        finish_kernel,
        out_shape=shape((node_rows, feat_width), BF16),
        in_specs=[in_vmem, in_vmem, anywhere],
        out_specs=in_vmem,
        scratch_shapes=[
            VMEM((near, feat_width, own_hidden), BF16),
            VMEM((near, feat_width, own_hidden), BF16),
            dma(2),
        ],
        compiler_params=grant(8),
        name="finish",
    )(vmem(partial), vmem(normed), w_far)


def solution(mesh):
    group, dom = mesh.devices.shape
    fine = Mesh(mesh.devices.reshape(group // 2, 2, dom // 4, 4), AXES)
    placed = (
        P(AXES, None),
        P(AXES, None),
        P(AXES, None),
        P(AXES, None),
        P(),
        P(None, ("x", "c")),
        P(None, ("x", "c")),
        P(),
        P(AXES, None),
        P(AXES),
    )
    return jax.shard_map(
        local, mesh=fine, in_specs=placed, out_specs=P(AXES, None), check_vma=False
    )
```
